32 devices in a mesh: prow: 4 (over x, core), pcol: 8 (over z, y).
Axes of the slice: x: 2, y: 2, z: 4, core: 2. Of those that a mesh axis runs over, the one named last changes fastest.
Arguments:
- sep_inverse: bfloat16 [2, 4, 256, 1, 8, 256], P(None, 'prow', None, None, 'pcol'), may hold values from -2 to 30, as said below
- panels: bfloat16 [4, 2, 4, 256, 256], P(None, None, 'prow', 'pcol'), may hold values from -0.125 to 0.125
- ancestors: int32 [4, 8], replicated, may hold values from 0 to 1, as said below
- window_factor: bfloat16 [6, 256, 256], replicated, may hold values from -0.1875 to 0.1875
- diag_inverse: bfloat16 [4, 256, 256], replicated, may hold values from -1 to 4, as said below
Outputs:
- ys: float32 [4, 2, 4, 256, 256], P(None, None, 'prow', 'pcol')
- window_inverse: float32 [1024, 1024], P('prow', 'pcol')
The draws below stay inside these ranges and needn't reach their ends.
Inputs may be any that keep to these rules, and one draw needn't show every extreme that they name: sep_inverse read as in the first step is symmetric. `diag_inverse`: each block is symmetric. ancestors[k + 1, t] <= ancestors[k, t]: a supernode's ancestor tiles lie among those of the one before it.
All inputs are finite; a program needn't handle non-finite values.
Results may differ from the reference program's by a relative error of at most 0.00035.
Values may be sent and summed in bfloat16 or wider, within the bound.
No kernel may reach another device: no remote copies, remote signals or barrier semaphores. Data moves between devices by JAX's collectives and lax.ppermute only.
A program may use at most 64 MiB of HBM per device.

```python
import math
import jax
import jax.numpy as jnp
from jax import lax

W = 256
KS = 4
RC = 2
NT = 8
CC = 1
SEP = 2048
PAIRS = 6
N_PROW = 4
N_PCOL = 8


def noise(key, shape):
    return jnp.clip(jax.random.normal(key, shape, jnp.float32), -4.0, 4.0)


def draw_sep_inverse(key, part):
    off_scale = 0.35 / math.sqrt(SEP * 2.0)
    lower_end, upper_end = (0.5, 1.5)

    def one_row(tile_row):

        def one_tile(tile_column):
            forward = noise(jax.random.fold_in(key, tile_row * NT + tile_column), (W, W))
            backward = noise(jax.random.fold_in(key, tile_column * NT + tile_row), (W, W))
            return (forward + backward.T) * off_scale
        row_tiles = jax.vmap(one_tile)(jnp.arange(NT, dtype=jnp.int32))
        diagonal_terms = jax.random.uniform(jax.random.fold_in(key, NT * NT + tile_row), (W,), jnp.float32, lower_end, upper_end)
        on_diagonal = (jnp.arange(NT, dtype=jnp.int32) == tile_row).astype(jnp.float32)[:, None, None]
        row_tiles = row_tiles + on_diagonal * jnp.diag(diagonal_terms)[None]
        return (16.0 * jnp.transpose(row_tiles, (1, 0, 2))).reshape(W, SEP).astype(jnp.bfloat16)
    row_blocks = lax.map(one_row, jnp.arange(NT, dtype=jnp.int32))
    return row_blocks.reshape(RC, N_PROW, W, CC, N_PCOL, W)


def draw_diag_inverse(key, part):
    raw_noise = noise(jax.random.fold_in(key, 7), (KS, W, W))
    identity = jnp.eye(W, dtype=jnp.float32)
    off_part = (raw_noise + jnp.transpose(raw_noise, (0, 2, 1))) * (0.6 / math.sqrt(2.0 * W)) * (1.0 - identity)[None]
    diagonal_terms = jax.random.uniform(jax.random.fold_in(key, 11), (KS, W), jnp.float32, 1.0, 3.0)
    return (off_part + identity[None] * diagonal_terms[:, None, :]).astype(jnp.bfloat16)


def draw_ancestors(key, part):
    levels = jax.random.randint(jax.random.fold_in(key, 3), (NT,), 0, KS + 2)
    return (levels[None, :] > jnp.arange(KS, dtype=jnp.int32)[:, None]).astype(jnp.int32)


def steps_of(own_key, dims, pieces, low, top_value):
    gain = 1.0
    for axis_at, parts in pieces:
        steps = jax.random.uniform(jax.random.fold_in(jax.random.fold_in(own_key, 6), axis_at), (parts,), jnp.float32, low / len(pieces), top_value / len(pieces))
        gain = gain * jnp.repeat(jnp.exp(steps), dims[axis_at] // parts).reshape((-1,) + (1,) * (len(dims) - 1 - axis_at))
    return gain


def normal_values(key, dims, width, most, cuts=(), kind=jnp.bfloat16):
    values = jax.random.normal(key, dims, jnp.float32) * width
    if len(cuts) > 0:
        values = steps_of(key, dims, cuts, -0.22, 0.18) * values
    return jnp.clip(values, min=-most, max=most).astype(kind)


def setup_inputs(seed: int = 0) -> dict:
    streams_of = jax.random.split(jax.random.key(seed), 6)
    return {
        "sep_inverse": draw_sep_inverse(jax.random.fold_in(streams_of[5], 71), 0),
        "panels": normal_values(streams_of[1], (KS, RC, N_PROW, W, W), SEP ** -0.5, 0.125, ((2, 4), (3, 8))),
        "ancestors": draw_ancestors(jax.random.fold_in(streams_of[5], 71), 0),
        "window_factor": normal_values(streams_of[3], (PAIRS, W, W), (KS * W) ** -0.5, 0.1875),
        "diag_inverse": draw_diag_inverse(jax.random.fold_in(streams_of[5], 71), 0),
    }


def product(operand_left, operand_right):
    return jnp.dot(operand_left, operand_right, precision=lax.Precision.HIGHEST, preferred_element_type=jnp.float32)


def pair_index(earlier, later):
    return later * (later - 1) // 2 + earlier


def window_step(later, window_sums, window_factor, diag_inverse, window_blocks):
    coupled = []
    for earlier in range(later):
        running = window_sums[earlier]
        for partner in range(later):
            running = running + product(window_blocks[(earlier, partner)], window_factor[pair_index(partner, later)].astype(jnp.float32))
        upper_block = -running
        window_blocks[(earlier, later)] = upper_block
        window_blocks[(later, earlier)] = upper_block.T
        coupled.append(upper_block)
    running = window_sums[later]
    for earlier in range(later):
        running = running + product(window_factor[pair_index(earlier, later)].astype(jnp.float32).T, coupled[earlier])
    window_blocks[(later, later)] = diag_inverse[later].astype(jnp.float32) - running


def assemble_window(window_blocks, supernodes):
    return jnp.block([[window_blocks[(first, second)] for second in range(supernodes)] for first in range(supernodes)])


def reference(sep_inverse, panels, ancestors, window_factor, diag_inverse):
    sep_columns = sep_inverse.reshape(SEP, CC, N_PCOL, W)
    window_blocks = {}
    columns = []
    for later in range(KS):
        row_keep = jnp.repeat(ancestors[later], W, total_repeat_length=SEP)
        factor = panels[later].reshape(SEP, W) * row_keep[:, None].astype(jnp.bfloat16)
        grouped = factor.reshape(CC, N_PCOL, W, W)

        def add_group(running_sum, column_group, grouped=grouped):
            sep_piece = lax.dynamic_index_in_dim(sep_columns, column_group, 2, keepdims=False).reshape(SEP, CC * W)
            factor_piece = lax.dynamic_index_in_dim(grouped, column_group, 1, keepdims=False).reshape(CC * W, W)
            partial_value = jnp.dot(sep_piece, factor_piece, preferred_element_type=jnp.float32)
            return running_sum + partial_value, None

        summed, _ = lax.scan(add_group, jnp.zeros((SEP, W), jnp.float32), jnp.arange(N_PCOL, dtype=jnp.int32))
        carried = -summed
        for earlier in range(later):
            carried = carried - product(columns[earlier], window_factor[pair_index(earlier, later)].astype(jnp.float32))
        current = carried * row_keep[:, None].astype(jnp.float32)
        factor_wide = factor.astype(jnp.float32)
        window_parts = [product(columns[earlier].T, factor_wide) for earlier in range(later)]
        window_parts.append(product(factor_wide.T, current))
        window_step(later, window_parts, window_factor, diag_inverse, window_blocks)
        columns.append(current)
    ys = jnp.stack(columns).reshape(KS, RC, N_PROW, W, W)
    return ys, assemble_window(window_blocks, KS)
```

```python
import functools

import jax
import jax.numpy as jnp
from jax import lax
from jax.experimental import pallas as pl
from jax.experimental.pallas import tpu as pltpu
from jax.sharding import PartitionSpec as P

AXES = ("prow", "pcol")
HIGHEST = lax.Precision.HIGHEST
VMEM = pl.BlockSpec(memory_space=pltpu.VMEM)
SMEM = pl.BlockSpec(memory_space=pltpu.SMEM)


def pair_index(earlier, later):
    return later * (later - 1) // 2 + earlier


def exact_dot(left, right):
    return jnp.dot(left, right, precision=HIGHEST, preferred_element_type=jnp.float32)


def dot(left, right):
    return jnp.dot(left, right, preferred_element_type=jnp.float32)


def dot_rows(left, right):
    return lax.dot_general(
        left, right, (((0,), (0,)), ((), ())), preferred_element_type=jnp.float32
    )


def split(value):
    high = value.astype(jnp.bfloat16)
    return high, (value - high.astype(jnp.float32)).astype(jnp.bfloat16)


def move(value, dx, dc, dz, dy):
    prow_count, pcol_count = (lax.axis_size(a) for a in AXES)
    flip_row, flip_col = 2 * dx + dc, 2 * dz + dy
    pairs = [
        (p * pcol_count + q, (p ^ flip_row) * pcol_count + (q ^ flip_col))
        for p in range(prow_count)
        for q in range(pcol_count)
    ]
    return lax.ppermute(value, AXES, pairs)


def inverse_blocks(window_factor, supernodes):
    factor = window_factor.astype(jnp.float32)
    blocks = {}
    for later in range(supernodes):
        for earlier in range(later):
            total = factor[pair_index(earlier, later)]
            for middle in range(earlier + 1, later):
                total = total + exact_dot(
                    blocks[earlier, middle], factor[pair_index(middle, later)]
                )
            blocks[earlier, later] = -total
    return blocks


def products_kernel(place_ref, flags_ref, *refs, pieces, supernodes, tile_rows, prow_count):
    panel_refs, inverse_ref = refs[:pieces], refs[pieces]
    high_ref, low_ref, panel_ref = refs[pieces + 1 :]
    prow, z = place_ref[0], place_ref[4]
    for later in range(supernodes):
        for r in range(tile_rows):
            keep = flags_ref[later, r * prow_count + prow].astype(jnp.float32)
            for d in range(pieces):
                panel_ref[later, r, lax.bitwise_xor(z, d)] = (
                    panel_refs[d][later, r].astype(jnp.float32) * keep
                )
    rows, width = high_ref.shape[1], high_ref.shape[2]
    panels = [panel_ref[k].reshape(rows, width) for k in range(supernodes)]
    for later in range(supernodes):
        total = panels[later]
        for earlier in range(later):
            total = total + exact_dot(panels[earlier], inverse_ref[pair_index(earlier, later)])
        high_ref[later], low_ref[later] = split(total)


def main_kernel(place_ref, flags_ref, *refs, lanes, pieces, supernodes, prow_count, width, steps):
    lane_refs, sep_refs = refs[:lanes], refs[lanes : lanes + pieces]
    high_ref, low_ref = refs[lanes + pieces : lanes + pieces + 2]
    column_refs = refs[lanes + pieces + 2 : lanes + 2 * pieces + 2]
    keep_ref, send_ref, gathered_ref, sums_ref, window_ref = refs[lanes + 2 * pieces + 2 :]
    prow, x, core, y, z = (place_ref[i] for i in range(5))
    _, tile_rows, sub_count, slice_rows, block = lane_refs[0].shape
    kind = gathered_ref.dtype
    for lane, (dx, dc, dy) in enumerate(steps):
        lane_prow = 2 * lax.bitwise_xor(x, dx) + lax.bitwise_xor(core, dc)
        parity = lax.bitwise_xor(y, dy)
        for half in range(2):
            for r in range(tile_rows):
                for sub in range(sub_count):
                    gathered_ref[half, r * prow_count + lane_prow, 2 * sub + parity] = lane_refs[
                        lane
                    ][half, r, sub].astype(kind)
    total = None
    for d in range(pieces):
        for dy in range(2):
            tile = 2 * lax.bitwise_xor(z, d) + lax.bitwise_xor(y, dy)
            sep = sep_refs[d][dy]
            for half in range(2):
                part = gathered_ref[half, tile].reshape(width, block).astype(jnp.bfloat16)
                term = dot(sep, part)
                total = term if total is None else total + term
    later = (z * block) // width
    sums_ref[...] = total.reshape(sums_ref.shape)
    for d in range(pieces):
        for r in range(tile_rows):
            keep = flags_ref[later, r * prow_count + prow].astype(jnp.float32)
            column_refs[d][r] = sums_ref[r, lax.bitwise_xor(z, d)] * -keep
    high, low = split(total)
    for k in range(supernodes):
        left_high, left_low = high_ref[k], low_ref[k]
        window_ref[k * width : (k + 1) * width, :] = (
            dot_rows(left_high, high) + dot_rows(left_high, low) + dot_rows(left_low, high)
        )
    x_count, _, rows_each, cols_each = keep_ref.shape
    for dx in range(x_count):
        for target, dc in ((keep_ref, 0), (send_ref, 1)):
            row_block = 2 * lax.bitwise_xor(x, dx) + lax.bitwise_xor(core, dc)
            rows = window_ref[pl.ds(pl.multiple_of(row_block * rows_each, rows_each), rows_each), :]
            first, second = rows[:, :cols_each], rows[:, cols_each:]
            target[dx, 0] = jnp.where(y == 0, first, second)
            target[dx, 1] = jnp.where(y == 0, second, first)


def add_kernel(keep_ref, received_ref, *out_refs):
    x_count = keep_ref.shape[0]
    for dx in range(x_count):
        for dy in range(2):
            out_refs[2 * dx + dy][...] = keep_ref[dx, dy] + received_ref[dx, dy]


def last_kernel(place_ref, *refs, parts, pieces):
    z = place_ref[4]
    part_refs, own_ref = refs[:parts], refs[parts]
    column_refs = refs[parts + 1 : parts + 1 + pieces]
    window_ref, ys_ref = refs[parts + 1 + pieces :]
    total = own_ref[...]
    for ref in part_refs:
        total = total + ref[...]
    window_ref[...] = total
    for d in range(pieces):
        ys_ref[lax.bitwise_xor(z, d)] = column_refs[d][...]


def call(kernel, operands, scalars, outs, scratch, flops):
    return pl.pallas_call(
        kernel,
        out_shape=outs,
        in_specs=[SMEM] * scalars + [VMEM] * (len(operands) - scalars),
        out_specs=[VMEM] * len(outs),
        scratch_shapes=scratch,
        compiler_params=pltpu.CompilerParams(vmem_limit_bytes=56 * 1024 * 1024),
        cost_estimate=pl.CostEstimate(flops=flops, bytes_accessed=1 << 20, transcendentals=0),
    )(*operands)


def per_device(sep_inverse, panels, ancestors, window_factor, diag_inverse):
    prow_count, pcol_count = (lax.axis_size(a) for a in AXES)
    prow, pcol = (lax.axis_index(a) for a in AXES)
    x_count, z_count = prow_count // 2, pcol_count // 2
    x, core, z, y = prow // 2, prow % 2, pcol // 2, pcol % 2
    tile_rows, width = sep_inverse.shape[0], sep_inverse.shape[2]
    supernodes, slice_rows = panels.shape[0], panels.shape[3]
    order = supernodes * width
    block = order // z_count
    rows_each, cols_each = order // prow_count, order // pcol_count
    rows = tile_rows * z_count * slice_rows
    bf16, f32 = jnp.bfloat16, jnp.float32
    shape = jax.ShapeDtypeStruct
    place = jnp.stack([prow, x, core, y, z]).astype(jnp.int32)

    own_panels = panels.reshape(supernodes, tile_rows, slice_rows, width)
    panel_pieces = [own_panels] + [move(own_panels, 0, 0, d, 0) for d in range(1, z_count)]
    by_parity = sep_inverse.reshape(tile_rows, z_count, 2, slice_rows, width)
    kept = lax.dynamic_index_in_dim(by_parity, y, 2, keepdims=False)
    given = move(lax.dynamic_index_in_dim(by_parity, 1 - y, 2, keepdims=False), 0, 0, 0, 1)
    own_sep = jnp.stack([kept, given]).reshape(2, rows, width)
    sep_pieces = [own_sep] + [move(own_sep, 0, 0, d, 0) for d in range(1, z_count)]

    inverse = inverse_blocks(window_factor, supernodes)
    stacked = jnp.stack([inverse[m, k] for k in range(supernodes) for m in range(k)])
    whole = jnp.block(
        [
            [
                jnp.eye(width, dtype=f32)
                if m == k
                else inverse[m, k]
                if m < k
                else jnp.zeros((width, width), f32)
                for k in range(supernodes)
            ]
            for m in range(supernodes)
        ]
    )
    row_side = lax.dynamic_slice_in_dim(whole, prow * rows_each, rows_each, 1)
    col_side = lax.dynamic_slice_in_dim(whole, pcol * cols_each, cols_each, 1)
    scaled = jnp.einsum(
        "kab,kbc->kac",
        diag_inverse.astype(f32),
        col_side.reshape(supernodes, width, cols_each),
        precision=HIGHEST,
        preferred_element_type=f32,
    ).reshape(order, cols_each)
    own_window = exact_dot(row_side.T, scaled)

    high, low = call(
        functools.partial(
            products_kernel,
            pieces=z_count,
            supernodes=supernodes,
            tile_rows=tile_rows,
            prow_count=prow_count,
        ),
        [place, ancestors, *panel_pieces, stacked],
        2,
        [shape((supernodes, rows, width), bf16)] * 2,
        [pltpu.VMEM((supernodes, tile_rows, z_count, slice_rows, width), f32)],
        6 * rows * order * order,
    )
    both = jnp.stack([high, low])
    if block == width:
        mine = lax.dynamic_index_in_dim(both, z, 1, keepdims=False)
    else:
        chosen = lax.dynamic_index_in_dim(both, (z * block) // width, 1, keepdims=False)
        mine = lax.dynamic_slice_in_dim(chosen, (z * block) % width, block, 2)
    mine = mine.reshape(2, tile_rows, z_count, slice_rows, block)
    steps, lanes = [], []
    for dx in range(x_count):
        for dy in range(2):
            lane = mine if dx + dy == 0 else move(mine, dx, 0, 0, dy)
            lanes.append(lane)
            steps.append((dx, 0, dy))
    for (dx, _, dy), lane in zip(list(steps), list(lanes)):
        lanes.append(move(lane, 0, 1, 0, 0))
        steps.append((dx, 1, dy))

    kind = bf16 if slice_rows % 16 == 0 else f32
    *columns, keep, send = call(
        functools.partial(
            main_kernel,
            lanes=len(lanes),
            pieces=z_count,
            supernodes=supernodes,
            prow_count=prow_count,
            width=width,
            steps=tuple(steps),
        ),
        [place, ancestors, *lanes, *sep_pieces, high, low],
        2,
        [shape((tile_rows, slice_rows, block), f32)] * z_count
        + [shape((x_count, 2, rows_each, cols_each), f32)] * 2,
        [
            pltpu.VMEM((2, tile_rows * prow_count, pcol_count, slice_rows, block), kind),
            pltpu.VMEM((tile_rows, z_count, slice_rows, block), f32),
            pltpu.VMEM((order, block), f32),
        ],
        4 * rows * block * (tile_rows * prow_count * width) + 6 * rows * block * order,
    )
    received = move(send, 0, 1, 0, 0)
    parts = call(
        add_kernel,
        [keep, received],
        0,
        [shape((rows_each, cols_each), f32)] * (2 * x_count),
        [],
        order * block,
    )
    column_pieces = [columns[0]] + [move(columns[d], 0, 0, d, 0) for d in range(1, z_count)]
    summed = [parts[0]] + [
        move(parts[2 * dx + dy], dx, 0, 0, dy)
        for dx in range(x_count)
        for dy in range(2)
        if dx + dy > 0
    ]
    window, ys = call(
        functools.partial(last_kernel, parts=len(summed), pieces=z_count),
        [place, *summed, own_window, *column_pieces],
        1,
        [
            shape((rows_each, cols_each), f32),
            shape((z_count, tile_rows, slice_rows, block), f32),
        ],
        [],
        order * block,
    )
    if block != width:
        ys = ys.reshape(supernodes, width // block, tile_rows, slice_rows, block)
        ys = jnp.transpose(ys, (0, 2, 3, 1, 4))
    return ys.reshape(supernodes, tile_rows, 1, slice_rows, width), window


def solution(mesh):
    placed = (
        P(None, "prow", None, None, "pcol", None),
        P(None, None, "prow", "pcol", None),
        P(),
        P(),
        P(),
    )
    return jax.shard_map(
        per_device,
        mesh=mesh,
        in_specs=placed,
        out_specs=(P(None, None, "prow", "pcol", None), P("prow", "pcol")),
        check_vma=False,
    )
```

```python
import functools

import jax
import jax.numpy as jnp
from jax import lax
from jax.experimental import pallas as pl
from jax.experimental.pallas import tpu as pltpu
from jax.sharding import PartitionSpec as P

AXES = ("prow", "pcol")
HIGHEST = lax.Precision.HIGHEST
VMEM = pl.BlockSpec(memory_space=pltpu.VMEM)
SMEM = pl.BlockSpec(memory_space=pltpu.SMEM)


def pair_index(earlier, later):
    return later * (later - 1) // 2 + earlier


def exact_dot(left, right):
    return jnp.dot(left, right, precision=HIGHEST, preferred_element_type=jnp.float32)


def dot(left, right):
    return jnp.dot(left, right, preferred_element_type=jnp.float32)


def dot_rows(left, right):
    return lax.dot_general(
        left, right, (((0,), (0,)), ((), ())), preferred_element_type=jnp.float32
    )


def split(value):
    high = value.astype(jnp.bfloat16)
    return high, (value - high.astype(jnp.float32)).astype(jnp.bfloat16)


def move(value, dx, dc, dz, dy):
    prow_count, pcol_count = (lax.axis_size(a) for a in AXES)
    flip_row, flip_col = 2 * dx + dc, 2 * dz + dy
    pairs = [
        (p * pcol_count + q, (p ^ flip_row) * pcol_count + (q ^ flip_col))
        for p in range(prow_count)
        for q in range(pcol_count)
    ]
    return lax.ppermute(value, AXES, pairs)


def exact_dot_rows(left, right):
    return lax.dot_general(
        left,
        right,
        (((0,), (0,)), ((), ())),
        precision=HIGHEST,
        preferred_element_type=jnp.float32,
    )


def inverse_kernel(place_ref, factor_ref, diag_ref, inverse_ref, own_ref, full_ref, rows_ref):
    prow, pcol = place_ref[0], place_ref[5]
    supernodes, width, _ = diag_ref.shape
    rows_each, cols_each = own_ref.shape
    square = (width, width)
    on_diagonal = lax.broadcasted_iota(jnp.int32, square, 0) == lax.broadcasted_iota(
        jnp.int32, square, 1
    )
    for later in range(supernodes):
        for earlier in range(supernodes):
            if earlier == later:
                full_ref[earlier, later] = on_diagonal.astype(jnp.float32)
            elif earlier > later:
                full_ref[earlier, later] = jnp.zeros(square, jnp.float32)
            else:
                total = factor_ref[pair_index(earlier, later)].astype(jnp.float32)
                for middle in range(earlier + 1, later):
                    total = total + exact_dot(
                        full_ref[earlier, middle],
                        factor_ref[pair_index(middle, later)].astype(jnp.float32),
                    )
                full_ref[earlier, later] = -total
                inverse_ref[pair_index(earlier, later)] = -total
    row_node, col_node = prow * rows_each // width, pcol * cols_each // width

    rows_ref[...] = jnp.zeros(square, jnp.float32)

    @pl.loop(0, jnp.minimum(row_node, col_node) + 1)
    def _(k):
        scaled = exact_dot(diag_ref[k].astype(jnp.float32), full_ref[k, col_node])
        rows_ref[...] += exact_dot_rows(full_ref[k, row_node], scaled)

    first_row = pl.multiple_of(prow * rows_each % width, rows_each)
    rows = rows_ref[pl.ds(first_row, rows_each), :]
    picked = lax.broadcasted_iota(jnp.int32, (width, cols_each), 0) == (
        lax.broadcasted_iota(jnp.int32, (width, cols_each), 1) + pcol * cols_each % width
    )
    own_ref[...] = exact_dot(rows, picked.astype(jnp.float32))


def products_kernel(place_ref, flags_ref, *refs, pieces, supernodes, tile_rows, prow_count):
    panel_refs, inverse_ref = refs[:pieces], refs[pieces]
    high_ref, low_ref, *mine_refs, panel_ref = refs[pieces + 1 :]
    prow, z = place_ref[0], place_ref[4]
    for later in range(supernodes):
        for r in range(tile_rows):
            keep = flags_ref[later, r * prow_count + prow].astype(jnp.float32)
            for d in range(pieces):
                panel_ref[later, r, lax.bitwise_xor(z, d)] = (
                    panel_refs[d][later, r].astype(jnp.float32) * keep
                )
    rows, width = high_ref.shape[1], high_ref.shape[2]
    panels = [panel_ref[k].reshape(rows, width) for k in range(supernodes)]
    for later in range(supernodes):
        total = panels[later]
        for earlier in range(later):
            total = total + exact_dot(panels[earlier], inverse_ref[pair_index(earlier, later)])
        high_ref[later], low_ref[later] = split(total)
    for mine_ref in mine_refs:
        mine_ref[0], mine_ref[1] = high_ref[z], low_ref[z]


def main_kernel(place_ref, flags_ref, *refs, lanes, pieces, supernodes, prow_count, width, steps):
    lane_refs, sep_refs = refs[:lanes], refs[lanes : lanes + pieces]
    high_ref, low_ref = refs[lanes + pieces : lanes + pieces + 2]
    column_refs = refs[lanes + pieces + 2 : lanes + 2 * pieces + 2]
    keep_ref, send_ref, gathered_ref, sums_ref, window_ref = refs[lanes + 2 * pieces + 2 :]
    prow, x, core, y, z = (place_ref[i] for i in range(5))
    _, tile_rows, sub_count, slice_rows, block = lane_refs[0].shape
    kind = gathered_ref.dtype
    for lane, (dx, dc, dy) in enumerate(steps):
        lane_prow = 2 * lax.bitwise_xor(x, dx) + lax.bitwise_xor(core, dc)
        parity = lax.bitwise_xor(y, dy)
        for half in range(2):
            for r in range(tile_rows):
                for sub in range(sub_count):
                    gathered_ref[half, r * prow_count + lane_prow, 2 * sub + parity] = lane_refs[
                        lane
                    ][half, r, sub].astype(kind)
    total = None
    for d in range(pieces):
        for dy in range(2):
            tile = 2 * lax.bitwise_xor(z, d) + lax.bitwise_xor(y, dy)
            sep = sep_refs[d][dy]
            for half in range(2):
                part = gathered_ref[half, tile].reshape(width, block).astype(jnp.bfloat16)
                term = dot(sep, part)
                total = term if total is None else total + term
    later = (z * block) // width
    sums_ref[...] = total.reshape(sums_ref.shape)
    for d in range(pieces):
        for r in range(tile_rows):
            keep = flags_ref[later, r * prow_count + prow].astype(jnp.float32)
            column_refs[d][r] = sums_ref[r, lax.bitwise_xor(z, d)] * -keep
    high, low = split(total)
    for k in range(supernodes):
        left_high, left_low = high_ref[k], low_ref[k]
        window_ref[k * width : (k + 1) * width, :] = (
            dot_rows(left_high, high) + dot_rows(left_high, low) + dot_rows(left_low, high)
        )
    x_count, _, rows_each, cols_each = keep_ref.shape
    for dx in range(x_count):
        for target, dc in ((keep_ref, 0), (send_ref, 1)):
            row_block = 2 * lax.bitwise_xor(x, dx) + lax.bitwise_xor(core, dc)
            rows = window_ref[pl.ds(pl.multiple_of(row_block * rows_each, rows_each), rows_each), :]
            first, second = rows[:, :cols_each], rows[:, cols_each:]
            target[dx, 0] = jnp.where(y == 0, first, second)
            target[dx, 1] = jnp.where(y == 0, second, first)


def add_kernel(keep_ref, received_ref, *out_refs):
    x_count = keep_ref.shape[0]
    for dx in range(x_count):
        for dy in range(2):
            out_refs[2 * dx + dy][...] = keep_ref[dx, dy] + received_ref[dx, dy]


def last_kernel(place_ref, *refs, parts, pieces):
    z = place_ref[4]
    part_refs, own_ref = refs[:parts], refs[parts]
    column_refs = refs[parts + 1 : parts + 1 + pieces]
    window_ref, ys_ref = refs[parts + 1 + pieces :]
    total = own_ref[...]
    for ref in part_refs:
        total = total + ref[...]
    window_ref[...] = total
    for d in range(pieces):
        ys_ref[lax.bitwise_xor(z, d)] = column_refs[d][...]


def call(kernel, operands, scalars, outs, scratch):
    arrays = [pltpu.with_memory_space_constraint(a, pltpu.VMEM) for a in operands[scalars:]]
    return pl.pallas_call(
        kernel,
        out_shape=[pltpu.VMEM(out.shape, out.dtype) for out in outs],
        in_specs=[SMEM] * scalars + [VMEM] * len(arrays),
        out_specs=[VMEM] * len(outs),
        scratch_shapes=scratch,
        compiler_params=pltpu.CompilerParams(vmem_limit_bytes=20 * 1024 * 1024),
        cost_estimate=pl.CostEstimate(flops=0, bytes_accessed=0, transcendentals=0),
    )(*operands[:scalars], *arrays)


def per_device(sep_inverse, panels, ancestors, window_factor, diag_inverse):
    prow_count, pcol_count = (lax.axis_size(a) for a in AXES)
    prow, pcol = (lax.axis_index(a) for a in AXES)
    x_count, z_count = prow_count // 2, pcol_count // 2
    x, core, z, y = prow // 2, prow % 2, pcol // 2, pcol % 2
    tile_rows, width = sep_inverse.shape[0], sep_inverse.shape[2]
    supernodes, slice_rows = panels.shape[0], panels.shape[3]
    order = supernodes * width
    block = order // z_count
    rows_each, cols_each = order // prow_count, order // pcol_count
    rows = tile_rows * z_count * slice_rows
    bf16, f32 = jnp.bfloat16, jnp.float32
    shape = jax.ShapeDtypeStruct
    place = jnp.stack([prow, x, core, y, z, pcol]).astype(jnp.int32)

    own_panels = panels.reshape(supernodes, tile_rows, slice_rows, width)
    panel_pieces = [own_panels] + [move(own_panels, 0, 0, d, 0) for d in range(1, z_count)]
    by_parity = sep_inverse.reshape(tile_rows, z_count, 2, slice_rows, width)
    kept = lax.dynamic_index_in_dim(by_parity, y, 2, keepdims=False)
    given = move(lax.dynamic_index_in_dim(by_parity, 1 - y, 2, keepdims=False), 0, 0, 0, 1)
    own_sep = jnp.stack([kept, given]).reshape(2, rows, width)
    sep_pieces = [own_sep] + [move(own_sep, 0, 0, d, 0) for d in range(1, z_count)]

    stacked, own_window = call(
        inverse_kernel,
        [place, window_factor, diag_inverse],
        1,
        [shape(window_factor.shape, f32), shape((rows_each, cols_each), f32)],
        [
            pltpu.VMEM((supernodes, supernodes, width, width), f32),
            pltpu.VMEM((width, width), f32),
        ],
    )

    high, low, *mine = call(
        functools.partial(
            products_kernel,
            pieces=z_count,
            supernodes=supernodes,
            tile_rows=tile_rows,
            prow_count=prow_count,
        ),
        [place, ancestors, *panel_pieces, stacked],
        2,
        [shape((supernodes, rows, width), bf16)] * 2
        + [shape((2, rows, width), bf16)] * (block == width),
        [pltpu.VMEM((supernodes, tile_rows, z_count, slice_rows, width), f32)],
    )
    if block == width:
        mine = mine[0]
    else:
        both = jnp.stack([high, low])
        chosen = lax.dynamic_index_in_dim(both, (z * block) // width, 1, keepdims=False)
        mine = lax.dynamic_slice_in_dim(chosen, (z * block) % width, block, 2)
    mine = mine.reshape(2, tile_rows, z_count, slice_rows, block)
    steps, lanes = [], []
    for dx in range(x_count):
        for dy in range(2):
            lane = mine if dx + dy == 0 else move(mine, dx, 0, 0, dy)
            lanes.append(lane)
            steps.append((dx, 0, dy))
    for (dx, _, dy), lane in zip(list(steps), list(lanes)):
        lanes.append(move(lane, 0, 1, 0, 0))
        steps.append((dx, 1, dy))

    kind = bf16 if slice_rows % 16 == 0 else f32
    *columns, keep, send = call(
        functools.partial(
            main_kernel,
            lanes=len(lanes),
            pieces=z_count,
            supernodes=supernodes,
            prow_count=prow_count,
            width=width,
            steps=tuple(steps),
        ),
        [place, ancestors, *lanes, *sep_pieces, high, low],
        2,
        [shape((tile_rows, slice_rows, block), f32)] * z_count
        + [shape((x_count, 2, rows_each, cols_each), f32)] * 2,
        [
            pltpu.VMEM((2, tile_rows * prow_count, pcol_count, slice_rows, block), kind),
            pltpu.VMEM((tile_rows, z_count, slice_rows, block), f32),
            pltpu.VMEM((order, block), f32),
        ],
    )
    received = move(send, 0, 1, 0, 0)
    parts = call(
        add_kernel,
        [keep, received],
        0,
        [shape((rows_each, cols_each), f32)] * (2 * x_count),
        [],
    )
    column_pieces = [columns[0]] + [move(columns[d], 0, 0, d, 0) for d in range(1, z_count)]
    summed = [parts[0]] + [
        move(parts[2 * dx + dy], dx, 0, 0, dy)
        for dx in range(x_count)
        for dy in range(2)
        if dx + dy > 0
    ]
    window, ys = call(
        functools.partial(last_kernel, parts=len(summed), pieces=z_count),
        [place, *summed, own_window, *column_pieces],
        1,
        [
            shape((rows_each, cols_each), f32),
            shape((z_count, tile_rows, slice_rows, block), f32),
        ],
        [],
    )
    if block != width:
        ys = ys.reshape(supernodes, width // block, tile_rows, slice_rows, block)
        ys = jnp.transpose(ys, (0, 2, 3, 1, 4))
    return ys.reshape(supernodes, tile_rows, 1, slice_rows, width), window


def solution(mesh):
    placed = (
        P(None, "prow", None, None, "pcol", None),
        P(None, None, "prow", "pcol", None),
        P(),
        P(),
        P(),
    )
    return jax.shard_map(
        per_device,
        mesh=mesh,
        in_specs=placed,
        out_specs=(P(None, None, "prow", "pcol", None), P("prow", "pcol")),
        check_vma=False,
    )
```

```python
import functools

import jax
import jax.numpy as jnp
from jax import lax
from jax.experimental import pallas as pl
from jax.experimental.pallas import tpu as pltpu
from jax.sharding import PartitionSpec as P

AXES = ("prow", "pcol")
HIGHEST = lax.Precision.HIGHEST
VMEM = pl.BlockSpec(memory_space=pltpu.VMEM)
SMEM = pl.BlockSpec(memory_space=pltpu.SMEM)


def pair_index(earlier, later):
    return later * (later - 1) // 2 + earlier


def exact_dot(left, right):
    return jnp.dot(left, right, precision=HIGHEST, preferred_element_type=jnp.float32)


def dot(left, right):
    return jnp.dot(left, right, preferred_element_type=jnp.float32)


def dot_rows(left, right):
    return lax.dot_general(
        left, right, (((0,), (0,)), ((), ())), preferred_element_type=jnp.float32
    )


def split(value):
    high = value.astype(jnp.bfloat16)
    return high, (value - high.astype(jnp.float32)).astype(jnp.bfloat16)


def move(value, dx, dc, dz, dy):
    prow_count, pcol_count = (lax.axis_size(a) for a in AXES)
    flip_row, flip_col = 2 * dx + dc, 2 * dz + dy
    pairs = [
        (p * pcol_count + q, (p ^ flip_row) * pcol_count + (q ^ flip_col))
        for p in range(prow_count)
        for q in range(pcol_count)
    ]
    return lax.ppermute(value, AXES, pairs)


def exact_dot_rows(left, right):
    return lax.dot_general(
        left,
        right,
        (((0,), (0,)), ((), ())),
        precision=HIGHEST,
        preferred_element_type=jnp.float32,
    )


def three_parts(value):
    high, rest = split(value)
    low = (value - high.astype(jnp.float32) - rest.astype(jnp.float32)).astype(jnp.bfloat16)
    return high, rest, low


def inverse_kernel(factor_ref, inverse_ref, *, supernodes):
    for later in range(supernodes):
        for earlier in range(later):
            total = factor_ref[pair_index(earlier, later)].astype(jnp.float32)
            for middle in range(earlier + 1, later):
                right = factor_ref[pair_index(middle, later)]
                for part in three_parts(inverse_ref[pair_index(earlier, middle)]):
                    total = total + dot(part, right)
            inverse_ref[pair_index(earlier, later)] = -total


def diagonal_kernel(place_ref, inverse_ref, diag_ref, own_ref, full_ref, rows_ref):
    prow, pcol = place_ref[0], place_ref[5]
    supernodes, width, _ = diag_ref.shape
    rows_each, cols_each = own_ref.shape
    row_node, col_node = prow * rows_each // width, pcol * cols_each // width
    square = (width, width)
    on_diagonal = lax.broadcasted_iota(jnp.int32, square, 0) == lax.broadcasted_iota(
        jnp.int32, square, 1
    )
    for which, node in enumerate((row_node, col_node)):
        full_ref[which, node] = on_diagonal.astype(jnp.float32)

        @pl.loop(0, node)
        def _(k, which=which, node=node):
            full_ref[which, k] = inverse_ref[node * (node - 1) // 2 + k]

    halves = 2 * cols_each == width
    rows_ref[...] = jnp.zeros_like(rows_ref)

    @pl.loop(0, jnp.minimum(row_node, col_node) + 1)
    def _(k):
        cols = full_ref[1, k]
        if halves:
            cols = jnp.where(pcol % 2 == 0, cols[:, :cols_each], cols[:, cols_each:])
        scaled = sum(dot(diag_ref[k], part) for part in three_parts(cols))
        rows_ref[...] += exact_dot_rows(full_ref[0, k], scaled)

    first_row = pl.multiple_of(prow * rows_each % width, rows_each)
    rows = rows_ref[pl.ds(first_row, rows_each), :]
    if not halves:
        picked = lax.broadcasted_iota(jnp.int32, (width, cols_each), 0) == (
            lax.broadcasted_iota(jnp.int32, (width, cols_each), 1) + pcol * cols_each % width
        )
        rows = exact_dot(rows, picked.astype(jnp.float32))
    own_ref[...] = rows


def products_kernel(place_ref, flags_ref, *refs, pieces, supernodes, tile_rows, prow_count):
    panel_refs, inverse_ref = refs[:pieces], refs[pieces]
    high_ref, low_ref, *mine_refs, panel_ref = refs[pieces + 1 :]
    prow, z = place_ref[0], place_ref[4]
    for later in range(supernodes):
        for r in range(tile_rows):
            keep = flags_ref[later, r * prow_count + prow].astype(jnp.float32)
            for d in range(pieces):
                panel_ref[later, r, lax.bitwise_xor(z, d)] = (
                    panel_refs[d][later, r].astype(jnp.float32) * keep
                )
    rows, width = high_ref.shape[1], high_ref.shape[2]
    panels = [panel_ref[k].reshape(rows, width) for k in range(supernodes)]
    narrow = [panel.astype(jnp.bfloat16) for panel in panels]
    for later in range(supernodes):
        total = panels[later]
        for earlier in range(later):
            for part in three_parts(inverse_ref[pair_index(earlier, later)]):
                total = total + dot(narrow[earlier], part)
        high_ref[later], low_ref[later] = split(total)
    for mine_ref in mine_refs:
        mine_ref[0], mine_ref[1] = high_ref[z], low_ref[z]


def columns_kernel(place_ref, flags_ref, *refs, lanes, pieces, prow_count, width, steps):
    lane_refs, sep_refs = refs[:lanes], refs[lanes : lanes + pieces]
    column_refs = refs[lanes + pieces : lanes + 2 * pieces]
    high_ref, low_ref, gathered_ref, sums_ref = refs[lanes + 2 * pieces :]
    prow, x, core, y, z = (place_ref[i] for i in range(5))
    _, tile_rows, sub_count, slice_rows, block = lane_refs[0].shape
    kind = gathered_ref.dtype
    for lane, (dx, dc, dy) in enumerate(steps):
        lane_prow = 2 * lax.bitwise_xor(x, dx) + lax.bitwise_xor(core, dc)
        parity = lax.bitwise_xor(y, dy)
        for half in range(2):
            for r in range(tile_rows):
                for sub in range(sub_count):
                    gathered_ref[half, r * prow_count + lane_prow, 2 * sub + parity] = lane_refs[
                        lane
                    ][half, r, sub].astype(kind)
    total = None
    for d in range(pieces):
        for dy in range(2):
            tile = 2 * lax.bitwise_xor(z, d) + lax.bitwise_xor(y, dy)
            sep = sep_refs[d][dy]
            for half in range(2):
                part = gathered_ref[half, tile].reshape(width, block).astype(jnp.bfloat16)
                term = dot(sep, part)
                total = term if total is None else total + term
    later = (z * block) // width
    sums_ref[...] = total.reshape(sums_ref.shape)
    for d in range(pieces):
        for r in range(tile_rows):
            keep = flags_ref[later, r * prow_count + prow].astype(jnp.float32)
            column_refs[d][r] = sums_ref[r, lax.bitwise_xor(z, d)] * -keep
    high_ref[...], low_ref[...] = split(total)


def window_kernel(
    place_ref, left_high_ref, left_low_ref, high_ref, low_ref, keep_ref, send_ref, window_ref
):
    x, core, y = (place_ref[i] for i in range(1, 4))
    supernodes, _, width = left_high_ref.shape
    high, low = high_ref[...], low_ref[...]
    for k in range(supernodes):
        left_high, left_low = left_high_ref[k], left_low_ref[k]
        window_ref[k * width : (k + 1) * width, :] = (
            dot_rows(left_high, high) + dot_rows(left_high, low) + dot_rows(left_low, high)
        )
    x_count, _, rows_each, cols_each = keep_ref.shape
    for dx in range(x_count):
        for target, dc in ((keep_ref, 0), (send_ref, 1)):
            row_block = 2 * lax.bitwise_xor(x, dx) + lax.bitwise_xor(core, dc)
            rows = window_ref[pl.ds(pl.multiple_of(row_block * rows_each, rows_each), rows_each), :]
            first, second = rows[:, :cols_each], rows[:, cols_each:]
            target[dx, 0] = jnp.where(y == 0, first, second)
            target[dx, 1] = jnp.where(y == 0, second, first)


def add_kernel(keep_ref, received_ref, *out_refs):
    x_count = keep_ref.shape[0]
    for dx in range(x_count):
        for dy in range(2):
            out_refs[2 * dx + dy][...] = keep_ref[dx, dy] + received_ref[dx, dy]


def last_kernel(_, *refs):
    *part_refs, window_ref = refs
    total = part_refs[0][...]
    for ref in part_refs[1:]:
        total = total + ref[...]
    window_ref[...] = total


def ys_kernel(place_ref, *refs):
    *column_refs, ys_ref, done_ref = refs
    z = place_ref[4]
    for d, ref in enumerate(column_refs):
        ys_ref[lax.bitwise_xor(z, d)] = ref[...]
    done_ref[...] = jnp.zeros_like(done_ref)


def after(value, *others):
    return lax.optimization_barrier((value, *others))[0]


def call(kernel, operands, scalars, outs, scratch, cost, last=False):
    arrays = [pltpu.with_memory_space_constraint(a, pltpu.VMEM) for a in operands[scalars:]]
    return pl.pallas_call(
        kernel,
        out_shape=outs if last else [pltpu.VMEM(out.shape, out.dtype) for out in outs],
        in_specs=[SMEM] * scalars + [VMEM] * len(arrays),
        out_specs=[VMEM] * len(outs),
        scratch_shapes=scratch,
        compiler_params=pltpu.CompilerParams(vmem_limit_bytes=20 * 1024 * 1024),
        cost_estimate=pl.CostEstimate(flops=cost, bytes_accessed=0, transcendentals=0),
    )(*operands[:scalars], *arrays)


def per_device(sep_inverse, panels, ancestors, window_factor, diag_inverse):
    prow_count, pcol_count = (lax.axis_size(a) for a in AXES)
    prow, pcol = (lax.axis_index(a) for a in AXES)
    x_count, z_count = prow_count // 2, pcol_count // 2
    x, core, z, y = prow // 2, prow % 2, pcol // 2, pcol % 2
    tile_rows, width = sep_inverse.shape[0], sep_inverse.shape[2]
    supernodes, slice_rows = panels.shape[0], panels.shape[3]
    order = supernodes * width
    block = order // z_count
    rows_each, cols_each = order // prow_count, order // pcol_count
    rows = tile_rows * z_count * slice_rows
    bf16, f32 = jnp.bfloat16, jnp.float32
    shape = jax.ShapeDtypeStruct
    place = jnp.stack([prow, x, core, y, z, pcol]).astype(jnp.int32)

    own_panels = panels.reshape(supernodes, tile_rows, slice_rows, width)
    panel_pieces = [own_panels] + [move(own_panels, 0, 0, d, 0) for d in range(1, z_count)]
    local_sep = sep_inverse.reshape(tile_rows, width, width)
    both_sep = jnp.stack([local_sep, move(local_sep, 0, 0, 0, 1)])
    both_sep = both_sep.reshape(2, tile_rows, z_count, 2, slice_rows, width)
    own_sep = lax.dynamic_index_in_dim(both_sep, y, 3, keepdims=False).reshape(2, rows, width)
    sep_pieces = [own_sep] + [move(own_sep, 0, 0, d, 0) for d in range(1, z_count)]

    (stacked,) = call(
        functools.partial(inverse_kernel, supernodes=supernodes),
        [window_factor],
        0,
        [shape(window_factor.shape, f32)],
        [],
        cost=1_000_000_000,
    )
    (own_window,) = call(
        diagonal_kernel,
        [place, stacked, diag_inverse],
        1,
        [shape((rows_each, cols_each), f32)],
        [
            pltpu.VMEM((2, supernodes, width, width), f32),
            pltpu.VMEM((width, cols_each if 2 * cols_each == width else width), f32),
        ],
        cost=3_000_000_000,
    )

    high, low, *mine = call(
        functools.partial(
            products_kernel,
            pieces=z_count,
            supernodes=supernodes,
            tile_rows=tile_rows,
            prow_count=prow_count,
        ),
        [after(place, own_sep, own_window), ancestors, *panel_pieces, stacked],
        2,
        [shape((supernodes, rows, width), bf16)] * 2
        + [shape((2, rows, width), bf16)] * (block == width),
        [pltpu.VMEM((supernodes, tile_rows, z_count, slice_rows, width), f32)],
        cost=2_500_000_000,
    )
    if block == width:
        mine = mine[0]
    else:
        both = jnp.stack([high, low])
        chosen = lax.dynamic_index_in_dim(both, (z * block) // width, 1, keepdims=False)
        mine = lax.dynamic_slice_in_dim(chosen, (z * block) % width, block, 2)
    mine = mine.reshape(2, tile_rows, z_count, slice_rows, block)
    steps, lanes = [], []
    for dx in range(x_count):
        for dy in range(2):
            source = after(mine, sep_pieces[1]) if dx + dy == 2 else mine
            lane = mine if dx + dy == 0 else move(source, dx, 0, 0, dy)
            lanes.append(lane)
            steps.append((dx, 0, dy))
    for (dx, _, dy), lane in zip(list(steps), list(lanes)):
        lanes.append(move(lane, 0, 1, 0, 0))
        steps.append((dx, 1, dy))

    kind = bf16 if slice_rows % 16 == 0 else f32
    *columns, sums_high, sums_low = call(
        functools.partial(
            columns_kernel,
            lanes=len(lanes),
            pieces=z_count,
            prow_count=prow_count,
            width=width,
            steps=tuple(steps),
        ),
        [place, ancestors, *lanes, *sep_pieces],
        2,
        [shape((tile_rows, slice_rows, block), f32)] * z_count + [shape((rows, block), bf16)] * 2,
        [
            pltpu.VMEM((2, tile_rows * prow_count, pcol_count, slice_rows, block), kind),
            pltpu.VMEM((tile_rows, z_count, slice_rows, block), f32),
        ],
        cost=1_700_000_000,
    )
    column_pieces = [columns[0]] + [move(columns[d], 0, 0, d, 0) for d in range(1, z_count)]
    keep, send = call(
        window_kernel,
        [place, high, low, sums_high, sums_low],
        1,
        [shape((x_count, 2, rows_each, cols_each), f32)] * 2,
        [pltpu.VMEM((order, block), f32)],
        cost=1_400_000_000,
    )
    received = move(send, 0, 1, 0, 0)
    parts = call(
        add_kernel,
        [keep, received],
        0,
        [shape((rows_each, cols_each), f32)] * (2 * x_count),
        [],
        cost=100_000_000,
    )
    summed = [parts[0]] + [
        move(parts[2 * dx + dy], dx, 0, 0, dy)
        for dx in range(x_count)
        for dy in range(2)
        if dx + dy > 0
    ]
    ys, done = call(
        ys_kernel,
        [place, *column_pieces],
        1,
        [shape((z_count, tile_rows, slice_rows, block), f32), shape((8, 128), f32)],
        [],
        cost=12_000_000_000,
        last=True,
    )
    (window,) = call(
        last_kernel,
        [done, *summed, own_window],
        0,
        [shape((rows_each, cols_each), f32)],
        [],
        cost=500_000_000,
        last=True,
    )
    if block != width:
        ys = ys.reshape(supernodes, width // block, tile_rows, slice_rows, block)
        ys = jnp.transpose(ys, (0, 2, 3, 1, 4))
    return ys.reshape(supernodes, tile_rows, 1, slice_rows, width), window


def solution(mesh):
    placed = (
        P(None, "prow", None, None, "pcol", None),
        P(None, None, "prow", "pcol", None),
        P(),
        P(),
        P(),
    )
    return jax.shard_map(
        per_device,
        mesh=mesh,
        in_specs=placed,
        out_specs=(P(None, None, "prow", "pcol", None), P("prow", "pcol")),
        check_vma=False,
    )
```

```python
import functools

import jax
import jax.numpy as jnp
from jax import lax
from jax.experimental import pallas as pl
from jax.experimental.pallas import tpu as pltpu
from jax.sharding import PartitionSpec as P

AXES = ("prow", "pcol")
HIGHEST = lax.Precision.HIGHEST
VMEM = pl.BlockSpec(memory_space=pltpu.VMEM)
SMEM = pl.BlockSpec(memory_space=pltpu.SMEM)


def pair_index(earlier, later):
    return later * (later - 1) // 2 + earlier


def exact_dot(left, right):
    return jnp.dot(left, right, precision=HIGHEST, preferred_element_type=jnp.float32)


def dot(left, right):
    return jnp.dot(left, right, preferred_element_type=jnp.float32)


def dot_rows(left, right):
    return lax.dot_general(
        left, right, (((0,), (0,)), ((), ())), preferred_element_type=jnp.float32
    )


def split(value):
    high = value.astype(jnp.bfloat16)
    return high, (value - high.astype(jnp.float32)).astype(jnp.bfloat16)


def column_of(line, half):
    return 4 * (line // 2) + 2 * half + line % 2


def move(value, dx, dc, dl, dh):
    prow_count, pcol_count = (lax.axis_size(a) for a in AXES)
    flip_row, flip_col = 2 * dx + dc, column_of(dl, dh)
    pairs = [
        (p * pcol_count + q, (p ^ flip_row) * pcol_count + (q ^ flip_col))
        for p in range(prow_count)
        for q in range(pcol_count)
    ]
    return lax.ppermute(value, AXES, pairs)


def exact_dot_rows(left, right):
    return lax.dot_general(
        left,
        right,
        (((0,), (0,)), ((), ())),
        precision=HIGHEST,
        preferred_element_type=jnp.float32,
    )


def three_parts(value):
    high, rest = split(value)
    low = (value - high.astype(jnp.float32) - rest.astype(jnp.float32)).astype(jnp.bfloat16)
    return high, rest, low


def inverse_kernel(factor_ref, inverse_ref, *, supernodes):
    for later in range(supernodes):
        for earlier in range(later):
            total = factor_ref[pair_index(earlier, later)].astype(jnp.float32)
            for middle in range(earlier + 1, later):
                right = factor_ref[pair_index(middle, later)]
                for part in three_parts(inverse_ref[pair_index(earlier, middle)]):
                    total = total + dot(part, right)
            inverse_ref[pair_index(earlier, later)] = -total


def diagonal_kernel(place_ref, inverse_ref, diag_ref, own_ref, full_ref, rows_ref):
    prow, pcol = place_ref[0], place_ref[5]
    supernodes, width, _ = diag_ref.shape
    rows_each, cols_each = own_ref.shape
    row_node, col_node = prow * rows_each // width, pcol * cols_each // width
    square = (width, width)
    on_diagonal = lax.broadcasted_iota(jnp.int32, square, 0) == lax.broadcasted_iota(
        jnp.int32, square, 1
    )
    for which, node in enumerate((row_node, col_node)):
        full_ref[which, node] = on_diagonal.astype(jnp.float32)

        @pl.loop(0, node)
        def _(k, which=which, node=node):
            full_ref[which, k] = inverse_ref[node * (node - 1) // 2 + k]

    halves = 2 * cols_each == width
    rows_ref[...] = jnp.zeros_like(rows_ref)

    @pl.loop(0, jnp.minimum(row_node, col_node) + 1)
    def _(k):
        cols = full_ref[1, k]
        if halves:
            cols = jnp.where(pcol % 2 == 0, cols[:, :cols_each], cols[:, cols_each:])
        scaled = sum(dot(diag_ref[k], part) for part in three_parts(cols))
        rows_ref[...] += exact_dot_rows(full_ref[0, k], scaled)

    first_row = pl.multiple_of(prow * rows_each % width, rows_each)
    rows = rows_ref[pl.ds(first_row, rows_each), :]
    if not halves:
        picked = lax.broadcasted_iota(jnp.int32, (width, cols_each), 0) == (
            lax.broadcasted_iota(jnp.int32, (width, cols_each), 1) + pcol * cols_each % width
        )
        rows = exact_dot(rows, picked.astype(jnp.float32))
    own_ref[...] = rows


def products_kernel(place_ref, flags_ref, *refs, pieces, supernodes, tile_rows, prow_count):
    panel_refs, inverse_ref = refs[:pieces], refs[pieces]
    high_ref, low_ref, *mine_refs, panel_ref = refs[pieces + 1 :]
    prow, line = place_ref[0], place_ref[4]
    for later in range(supernodes):
        for r in range(tile_rows):
            keep = flags_ref[later, r * prow_count + prow].astype(jnp.float32)
            for d in range(pieces):
                panel_ref[later, r, lax.bitwise_xor(line, d)] = (
                    panel_refs[d][later, r].astype(jnp.float32) * keep
                )
    rows, width = high_ref.shape[1], high_ref.shape[2]
    panels = [panel_ref[k].reshape(rows, width) for k in range(supernodes)]
    narrow = [panel.astype(jnp.bfloat16) for panel in panels]
    for later in range(supernodes):
        total = panels[later]
        for earlier in range(later):
            for part in three_parts(inverse_ref[pair_index(earlier, later)]):
                total = total + dot(narrow[earlier], part)
        high_ref[later], low_ref[later] = split(total)
    for mine_ref in mine_refs:
        cols_each = width // 2
        first = line % 2 == 0
        for which, ref in enumerate((high_ref, low_ref)):
            for half in range(2):
                node = ref[column_of(line, half) // 2]
                mine_ref[which, :, half * cols_each : (half + 1) * cols_each] = jnp.where(
                    first, node[:, :cols_each], node[:, cols_each:]
                )


def columns_kernel(
    place_ref, flags_ref, *refs, lanes, pieces, lines, prow_count, width, steps, flips
):
    lane_refs, sep_refs = refs[:lanes], refs[lanes : lanes + pieces]
    column_refs = refs[lanes + pieces : lanes + pieces + lines]
    high_ref, low_ref, gathered_ref, sums_ref = refs[lanes + pieces + lines :]
    prow, x, core, half, line, pcol = (place_ref[i] for i in range(6))
    _, tile_rows, _, slice_rows, block = lane_refs[0].shape
    kind = gathered_ref.dtype
    for lane, (dx, dc, dh) in enumerate(steps):
        lane_prow = 2 * lax.bitwise_xor(x, dx) + lax.bitwise_xor(core, dc)
        lane_half = lax.bitwise_xor(half, dh)
        for which in range(2):
            for r in range(tile_rows):
                for sub in range(lines):
                    gathered_ref[
                        which, r * prow_count + lane_prow, column_of(sub, 0) + 2 * lane_half
                    ] = lane_refs[lane][which, r, sub].astype(kind)
    total = None
    for piece, flip in enumerate(flips):
        tile = lax.bitwise_xor(pcol, flip)
        sep = sep_refs[piece][...]
        for which in range(2):
            part = gathered_ref[which, tile].reshape(width, block).astype(jnp.bfloat16)
            term = dot(sep, part)
            total = term if total is None else total + term
    cols_each = block // 2
    nodes = [column_of(line, h) * cols_each // width for h in range(2)]
    sums_ref[...] = total.reshape(sums_ref.shape)
    first = lax.broadcasted_iota(jnp.int32, (slice_rows, block), 1) < cols_each
    for r in range(tile_rows):
        keeps = [flags_ref[k, r * prow_count + prow].astype(jnp.float32) for k in nodes]
        keep = jnp.where(first, -keeps[0], -keeps[1])
        for d in range(lines):
            column_refs[d][r] = sums_ref[r, lax.bitwise_xor(line, d)] * keep
    high_ref[...], low_ref[...] = split(total)


def window_kernel(
    place_ref, left_high_ref, left_low_ref, high_ref, low_ref, keep_ref, send_ref, window_ref
):
    x, core, half = (place_ref[i] for i in range(1, 4))
    supernodes, _, width = left_high_ref.shape
    high, low = high_ref[...], low_ref[...]
    for k in range(supernodes):
        left_high, left_low = left_high_ref[k], left_low_ref[k]
        window_ref[k * width : (k + 1) * width, :] = (
            dot_rows(left_high, high) + dot_rows(left_high, low) + dot_rows(left_low, high)
        )
    x_count, _, rows_each, cols_each = keep_ref.shape
    for dx in range(x_count):
        for target, dc in ((keep_ref, 0), (send_ref, 1)):
            row_block = 2 * lax.bitwise_xor(x, dx) + lax.bitwise_xor(core, dc)
            rows = window_ref[pl.ds(pl.multiple_of(row_block * rows_each, rows_each), rows_each), :]
            first, second = rows[:, :cols_each], rows[:, cols_each:]
            target[dx, 0] = jnp.where(half == 0, first, second)
            target[dx, 1] = jnp.where(half == 0, second, first)


def add_kernel(keep_ref, received_ref, *out_refs):
    x_count = keep_ref.shape[0]
    for dx in range(x_count):
        for dy in range(2):
            out_refs[2 * dx + dy][...] = keep_ref[dx, dy] + received_ref[dx, dy]


def last_kernel(_, *refs):
    *part_refs, window_ref = refs
    total = part_refs[0][...]
    for ref in part_refs[1:]:
        total = total + ref[...]
    window_ref[...] = total


def ys_kernel(place_ref, *refs):
    *column_refs, ys_ref, done_ref = refs
    done_ref[...] = jnp.zeros_like(done_ref)
    line = place_ref[4]
    block = column_refs[0].shape[2]
    cols_each = block // 2
    if ys_ref.ndim == 4 and ys_ref.shape[0] == len(column_refs) and ys_ref.shape[3] == block:
        first = line % 2 == 0
        for d in range(0, len(column_refs), 2):
            for half in range(2):
                node = column_of(lax.bitwise_xor(line, d), half) // 2
                cols = slice(half * cols_each, (half + 1) * cols_each)
                even, odd = column_refs[d][:, :, cols], column_refs[d + 1][:, :, cols]
                ys_ref[node, :, :, :cols_each] = jnp.where(first, even, odd)
                ys_ref[node, :, :, cols_each:] = jnp.where(first, odd, even)
    else:
        for d, ref in enumerate(column_refs):
            for half in range(2):
                ys_ref[lax.bitwise_xor(line, d), half] = ref[
                    :, :, half * cols_each : (half + 1) * cols_each
                ]


def after(value, *others):
    return lax.optimization_barrier((value, *others))[0]


def call(kernel, operands, scalars, outs, scratch, cost, last=False):
    arrays = [pltpu.with_memory_space_constraint(a, pltpu.VMEM) for a in operands[scalars:]]
    return pl.pallas_call(
        kernel,
        out_shape=outs if last else [pltpu.VMEM(out.shape, out.dtype) for out in outs],
        in_specs=[SMEM] * scalars + [VMEM] * len(arrays),
        out_specs=[VMEM] * len(outs),
        scratch_shapes=scratch,
        compiler_params=pltpu.CompilerParams(vmem_limit_bytes=20 * 1024 * 1024),
        cost_estimate=pl.CostEstimate(flops=cost, bytes_accessed=0, transcendentals=0),
    )(*operands[:scalars], *arrays)


def per_device(sep_inverse, panels, ancestors, window_factor, diag_inverse):
    prow_count, pcol_count = (lax.axis_size(a) for a in AXES)
    prow, pcol = (lax.axis_index(a) for a in AXES)
    x_count, lines = prow_count // 2, pcol_count // 2
    x, core, half = prow // 2, prow % 2, pcol // 2 % 2
    line = 2 * (pcol // 4) + pcol % 2
    tile_rows, width = sep_inverse.shape[0], sep_inverse.shape[2]
    supernodes, slice_rows = panels.shape[0], panels.shape[3]
    order = supernodes * width
    rows_each, cols_each = order // prow_count, order // pcol_count
    block = 2 * cols_each
    rows = tile_rows * lines * slice_rows
    bf16, f32 = jnp.bfloat16, jnp.float32
    shape = jax.ShapeDtypeStruct
    place = jnp.stack([prow, x, core, half, line, pcol]).astype(jnp.int32)

    own_panels = panels.reshape(supernodes, tile_rows, slice_rows, width)
    panel_pieces = []
    for dl in range(0, lines, 2):
        piece = own_panels if dl == 0 else move(own_panels, 0, 0, dl, 0)
        panel_pieces += [piece, move(piece, 0, 0, 1, 0)]
    by_half = sep_inverse.reshape(tile_rows, lines // 2, 2, 2, slice_rows, width)
    kept = lax.dynamic_index_in_dim(by_half, half, 2, keepdims=False).reshape(rows, width)
    given = lax.dynamic_index_in_dim(by_half, 1 - half, 2, keepdims=False).reshape(rows, width)
    sep_pieces, flips = [], []
    for dl in range(0, lines, 2):
        for dh in range(2):
            piece = kept if dl + dh == 0 else move((kept, given)[dh], 0, 0, dl, dh)
            sep_pieces += [piece, move(piece, 0, 0, 1, 0)]
            flips += [column_of(dl, dh), column_of(dl + 1, dh)]

    (stacked,) = call(
        functools.partial(inverse_kernel, supernodes=supernodes),
        [window_factor],
        0,
        [shape(window_factor.shape, f32)],
        [],
        cost=1_000_000_000,
    )
    (own_window,) = call(
        diagonal_kernel,
        [place, stacked, diag_inverse],
        1,
        [shape((rows_each, cols_each), f32)],
        [
            pltpu.VMEM((2, supernodes, width, width), f32),
            pltpu.VMEM((width, cols_each if 2 * cols_each == width else width), f32),
        ],
        cost=3_000_000_000,
    )

    high, low, *mine = call(
        functools.partial(
            products_kernel,
            pieces=lines,
            supernodes=supernodes,
            tile_rows=tile_rows,
            prow_count=prow_count,
        ),
        [after(place, own_window, sep_pieces[1], sep_pieces[3]), ancestors, *panel_pieces, stacked],
        2,
        [shape((supernodes, rows, width), bf16)] * 2
        + [shape((2, rows, block), bf16)] * (block == width),
        [pltpu.VMEM((supernodes, tile_rows, lines, slice_rows, width), f32)],
        cost=2_500_000_000,
    )
    if block == width:
        mine = mine[0]
    else:
        both = jnp.stack([high, low])
        slices = []
        for h in range(2):
            start = column_of(line, h) * cols_each
            chosen = lax.dynamic_index_in_dim(both, start // width, 1, keepdims=False)
            slices.append(lax.dynamic_slice_in_dim(chosen, start % width, cols_each, 2))
        mine = jnp.concatenate(slices, 2)
    mine = mine.reshape(2, tile_rows, lines, slice_rows, block)
    steps, lanes = [], []
    for dx in range(x_count):
        for dh in range(2):
            lane = mine if dx + dh == 0 else move(mine, dx, 0, 0, dh)
            lanes.append(lane)
            steps.append((dx, 0, dh))
    lanes[1:] = [after(lane, *sep_pieces[1:]) for lane in lanes[1:]]
    for (dx, _, dh), lane in zip(list(steps), list(lanes)):
        lanes.append(move(lane, 0, 1, 0, 0))
        steps.append((dx, 1, dh))

    kind = bf16 if slice_rows % 16 == 0 else f32
    *columns, sums_high, sums_low = call(
        functools.partial(
            columns_kernel,
            lanes=len(lanes),
            pieces=len(sep_pieces),
            lines=lines,
            prow_count=prow_count,
            width=width,
            steps=tuple(steps),
            flips=tuple(flips),
        ),
        [place, ancestors, *lanes, *sep_pieces],
        2,
        [shape((tile_rows, slice_rows, block), f32)] * lines + [shape((rows, block), bf16)] * 2,
        [
            pltpu.VMEM((2, tile_rows * prow_count, pcol_count, slice_rows, block), kind),
            pltpu.VMEM((tile_rows, lines, slice_rows, block), f32),
        ],
        cost=1_700_000_000,
    )
    column_pieces = [columns[0]] + [move(columns[d], 0, 0, d, 0) for d in range(1, lines)]
    keep, send = call(
        window_kernel,
        [place, high, low, sums_high, sums_low],
        1,
        [shape((x_count, 2, rows_each, cols_each), f32)] * 2,
        [pltpu.VMEM((order, block), f32)],
        cost=1_400_000_000,
    )
    received = move(send, 0, 1, 0, 0)
    parts = call(
        add_kernel,
        [keep, received],
        0,
        [shape((rows_each, cols_each), f32)] * (2 * x_count),
        [],
        cost=100_000_000,
    )
    by_node = block == width and lines == supernodes
    ys, done = call(
        ys_kernel,
        [place, *column_pieces],
        1,
        [
            shape((supernodes, tile_rows, slice_rows, width), f32)
            if by_node
            else shape((lines, 2, tile_rows, slice_rows, cols_each), f32),
            shape((8, 128), f32),
        ],
        [],
        cost=12_000_000_000,
        last=by_node,
    )
    if not by_node:
        ys = ys.reshape(lines // 2, 2, 2, tile_rows, slice_rows, cols_each)
        ys = jnp.transpose(ys, (3, 4, 0, 2, 1, 5))
        ys = ys.reshape(tile_rows, slice_rows, supernodes, width)
        ys = jnp.transpose(ys, (2, 0, 1, 3))
    summed = [parts[0]] + [
        move(parts[2 * dx + dh], dx, 0, 0, dh)
        for dx in range(x_count)
        for dh in range(2)
        if dx + dh > 0
    ]
    (window,) = call(
        last_kernel,
        [done, *summed, own_window],
        0,
        [shape((rows_each, cols_each), f32)],
        [],
        cost=500_000_000,
        last=True,
    )
    return ys.reshape(supernodes, tile_rows, 1, slice_rows, width), window


def solution(mesh):
    placed = (
        P(None, "prow", None, None, "pcol", None),
        P(None, None, "prow", "pcol", None),
        P(),
        P(),
        P(),
    )
    return jax.shard_map(
        per_device,
        mesh=mesh,
        in_specs=placed,
        out_specs=(P(None, None, "prow", "pcol", None), P("prow", "pcol")),
        check_vma=False,
    )
```

```python
import functools

import jax
import jax.numpy as jnp
from jax import lax
from jax.experimental import pallas as pl
from jax.experimental.pallas import tpu as pltpu
from jax.sharding import PartitionSpec as P

AXES = ("prow", "pcol")
HIGHEST = lax.Precision.HIGHEST
VMEM = pl.BlockSpec(memory_space=pltpu.VMEM)
SMEM = pl.BlockSpec(memory_space=pltpu.SMEM)


def pair_index(earlier, later):
    return later * (later - 1) // 2 + earlier


def exact_dot(left, right):
    return jnp.dot(left, right, precision=HIGHEST, preferred_element_type=jnp.float32)


def dot(left, right):
    return jnp.dot(left, right, preferred_element_type=jnp.float32)


def dot_rows(left, right):
    return lax.dot_general(
        left, right, (((0,), (0,)), ((), ())), preferred_element_type=jnp.float32
    )


def split(value):
    high = value.astype(jnp.bfloat16)
    return high, (value - high.astype(jnp.float32)).astype(jnp.bfloat16)


def column_of(line, half):
    return 4 * (line // 2) + 2 * half + line % 2


def move(value, dx, dc, dl, dh):
    prow_count, pcol_count = (lax.axis_size(a) for a in AXES)
    flip_row, flip_col = 2 * dx + dc, column_of(dl, dh)
    pairs = [
        (p * pcol_count + q, (p ^ flip_row) * pcol_count + (q ^ flip_col))
        for p in range(prow_count)
        for q in range(pcol_count)
    ]
    return lax.ppermute(value, AXES, pairs)


def exact_dot_rows(left, right):
    return lax.dot_general(
        left,
        right,
        (((0,), (0,)), ((), ())),
        precision=HIGHEST,
        preferred_element_type=jnp.float32,
    )


def three_parts(value):
    high, rest = split(value)
    low = (value - high.astype(jnp.float32) - rest.astype(jnp.float32)).astype(jnp.bfloat16)
    return high, rest, low


def inverse_kernel(factor_ref, inverse_ref, *, supernodes):
    for later in range(supernodes):
        for earlier in range(later):
            total = factor_ref[pair_index(earlier, later)].astype(jnp.float32)
            for middle in range(earlier + 1, later):
                right = factor_ref[pair_index(middle, later)]
                for part in three_parts(inverse_ref[pair_index(earlier, middle)]):
                    total = total + dot(part, right)
            inverse_ref[pair_index(earlier, later)] = -total


def diagonal_kernel(place_ref, inverse_ref, diag_ref, own_ref, full_ref, rows_ref):
    prow, pcol = place_ref[0], place_ref[5]
    supernodes, width, _ = diag_ref.shape
    rows_each, cols_each = own_ref.shape
    row_node, col_node = prow * rows_each // width, pcol * cols_each // width
    square = (width, width)
    on_diagonal = lax.broadcasted_iota(jnp.int32, square, 0) == lax.broadcasted_iota(
        jnp.int32, square, 1
    )
    for which, node in enumerate((row_node, col_node)):
        full_ref[which, node] = on_diagonal.astype(jnp.float32)

        @pl.loop(0, node)
        def _(k, which=which, node=node):
            full_ref[which, k] = inverse_ref[node * (node - 1) // 2 + k]

    halves = 2 * cols_each == width
    rows_ref[...] = jnp.zeros_like(rows_ref)

    @pl.loop(0, jnp.minimum(row_node, col_node) + 1)
    def _(k):
        cols = full_ref[1, k]
        if halves:
            cols = jnp.where(pcol % 2 == 0, cols[:, :cols_each], cols[:, cols_each:])
        scaled = sum(dot(diag_ref[k], part) for part in three_parts(cols))
        rows_ref[...] += exact_dot_rows(full_ref[0, k], scaled)

    first_row = pl.multiple_of(prow * rows_each % width, rows_each)
    rows = rows_ref[pl.ds(first_row, rows_each), :]
    if not halves:
        picked = lax.broadcasted_iota(jnp.int32, (width, cols_each), 0) == (
            lax.broadcasted_iota(jnp.int32, (width, cols_each), 1) + pcol * cols_each % width
        )
        rows = exact_dot(rows, picked.astype(jnp.float32))
    own_ref[...] = rows


def products_kernel(place_ref, flags_ref, *refs, pieces, supernodes, tile_rows, prow_count):
    panel_refs, inverse_ref = refs[:pieces], refs[pieces]
    high_ref, low_ref, *mine_refs, panel_ref = refs[pieces + 1 :]
    prow, line = place_ref[0], place_ref[4]
    for later in range(supernodes):
        for r in range(tile_rows):
            keep = flags_ref[later, r * prow_count + prow].astype(jnp.float32)
            for d in range(pieces):
                panel_ref[later, r, lax.bitwise_xor(line, d)] = (
                    panel_refs[d][later, r].astype(jnp.float32) * keep
                )
    rows, width = high_ref.shape[1], high_ref.shape[2]
    panels = [panel_ref[k].reshape(rows, width) for k in range(supernodes)]
    narrow = [panel.astype(jnp.bfloat16) for panel in panels]
    for later in range(supernodes):
        total = panels[later]
        for earlier in range(later):
            for part in split(inverse_ref[pair_index(earlier, later)]):
                total = total + dot(narrow[earlier], part)
        high_ref[later], low_ref[later] = split(total)
    for mine_ref in mine_refs:
        cols_each = width // 2
        first = line % 2 == 0
        for which, ref in enumerate((high_ref, low_ref)):
            for half in range(2):
                node = ref[column_of(line, half) // 2]
                mine_ref[which, :, half * cols_each : (half + 1) * cols_each] = jnp.where(
                    first, node[:, :cols_each], node[:, cols_each:]
                )


def columns_kernel(
    place_ref, flags_ref, *refs, lanes, pieces, lines, prow_count, width, steps, flips
):
    lane_refs, sep_refs = refs[:lanes], refs[lanes : lanes + pieces]
    column_refs = refs[lanes + pieces : lanes + pieces + lines]
    high_ref, low_ref, gathered_ref, sums_ref = refs[lanes + pieces + lines :]
    prow, x, core, half, line, pcol = (place_ref[i] for i in range(6))
    _, tile_rows, _, slice_rows, block = lane_refs[0].shape
    kind = gathered_ref.dtype
    for lane, (dx, dc, dh) in enumerate(steps):
        lane_prow = 2 * lax.bitwise_xor(x, dx) + lax.bitwise_xor(core, dc)
        lane_half = lax.bitwise_xor(half, dh)
        for which in range(2):
            for r in range(tile_rows):
                for sub in range(lines):
                    gathered_ref[
                        which, r * prow_count + lane_prow, column_of(sub, 0) + 2 * lane_half
                    ] = lane_refs[lane][which, r, sub].astype(kind)
    total = None
    for piece, flip in enumerate(flips):
        tile = lax.bitwise_xor(pcol, flip)
        sep = sep_refs[piece][...]
        for which in range(2):
            part = gathered_ref[which, tile].reshape(width, block).astype(jnp.bfloat16)
            term = dot(sep, part)
            total = term if total is None else total + term
    cols_each = block // 2
    nodes = [column_of(line, h) * cols_each // width for h in range(2)]
    sums_ref[...] = total.reshape(sums_ref.shape)
    first = lax.broadcasted_iota(jnp.int32, (slice_rows, block), 1) < cols_each
    for r in range(tile_rows):
        keeps = [flags_ref[k, r * prow_count + prow].astype(jnp.float32) for k in nodes]
        keep = jnp.where(first, -keeps[0], -keeps[1])
        for d in range(lines):
            column_refs[d][r] = sums_ref[r, lax.bitwise_xor(line, d)] * keep
    high_ref[...], low_ref[...] = split(total)


def window_kernel(
    place_ref, left_high_ref, left_low_ref, high_ref, low_ref, keep_ref, send_ref, window_ref
):
    x, core, half = (place_ref[i] for i in range(1, 4))
    supernodes, _, width = left_high_ref.shape
    high, low = high_ref[...], low_ref[...]
    for k in range(supernodes):
        left_high, left_low = left_high_ref[k], left_low_ref[k]
        window_ref[k * width : (k + 1) * width, :] = (
            dot_rows(left_high, high) + dot_rows(left_high, low) + dot_rows(left_low, high)
        )
    x_count, _, rows_each, cols_each = keep_ref.shape
    for dx in range(x_count):
        for target, dc in ((keep_ref, 0), (send_ref, 1)):
            row_block = 2 * lax.bitwise_xor(x, dx) + lax.bitwise_xor(core, dc)
            rows = window_ref[pl.ds(pl.multiple_of(row_block * rows_each, rows_each), rows_each), :]
            first, second = rows[:, :cols_each], rows[:, cols_each:]
            target[dx, 0] = jnp.where(half == 0, first, second)
            target[dx, 1] = jnp.where(half == 0, second, first)


def add_kernel(keep_ref, received_ref, *out_refs):
    x_count = keep_ref.shape[0]
    for dx in range(x_count):
        for dy in range(2):
            out_refs[2 * dx + dy][...] = keep_ref[dx, dy] + received_ref[dx, dy]


def last_kernel(_, *refs):
    *part_refs, window_ref = refs
    total = part_refs[0][...]
    for ref in part_refs[1:]:
        total = total + ref[...]
    window_ref[...] = total


def ys_kernel(place_ref, *refs):
    *column_refs, ys_ref, done_ref = refs
    done_ref[...] = jnp.zeros_like(done_ref)
    line = place_ref[4]
    block = column_refs[0].shape[2]
    cols_each = block // 2
    if ys_ref.ndim == 4 and ys_ref.shape[0] == len(column_refs) and ys_ref.shape[3] == block:
        first = line % 2 == 0
        for d in range(0, len(column_refs), 2):
            for half in range(2):
                node = column_of(lax.bitwise_xor(line, d), half) // 2
                cols = slice(half * cols_each, (half + 1) * cols_each)
                even, odd = column_refs[d][:, :, cols], column_refs[d + 1][:, :, cols]
                ys_ref[node, :, :, :cols_each] = jnp.where(first, even, odd)
                ys_ref[node, :, :, cols_each:] = jnp.where(first, odd, even)
    else:
        for d, ref in enumerate(column_refs):
            for half in range(2):
                ys_ref[lax.bitwise_xor(line, d), half] = ref[
                    :, :, half * cols_each : (half + 1) * cols_each
                ]


def after(value, *others):
    return lax.optimization_barrier((value, *others))[0]


def call(kernel, operands, scalars, outs, scratch, cost, last=False):
    arrays = [pltpu.with_memory_space_constraint(a, pltpu.VMEM) for a in operands[scalars:]]
    return pl.pallas_call(
        kernel,
        out_shape=outs if last else [pltpu.VMEM(out.shape, out.dtype) for out in outs],
        in_specs=[SMEM] * scalars + [VMEM] * len(arrays),
        out_specs=[VMEM] * len(outs),
        scratch_shapes=scratch,
        compiler_params=pltpu.CompilerParams(vmem_limit_bytes=20 * 1024 * 1024),
        cost_estimate=pl.CostEstimate(flops=cost, bytes_accessed=0, transcendentals=0),
    )(*operands[:scalars], *arrays)


def per_device(sep_inverse, panels, ancestors, window_factor, diag_inverse):
    prow_count, pcol_count = (lax.axis_size(a) for a in AXES)
    prow, pcol = (lax.axis_index(a) for a in AXES)
    x_count, lines = prow_count // 2, pcol_count // 2
    x, core, half = prow // 2, prow % 2, pcol // 2 % 2
    line = 2 * (pcol // 4) + pcol % 2
    tile_rows, width = sep_inverse.shape[0], sep_inverse.shape[2]
    supernodes, slice_rows = panels.shape[0], panels.shape[3]
    order = supernodes * width
    rows_each, cols_each = order // prow_count, order // pcol_count
    block = 2 * cols_each
    rows = tile_rows * lines * slice_rows
    bf16, f32 = jnp.bfloat16, jnp.float32
    shape = jax.ShapeDtypeStruct
    place = jnp.stack([prow, x, core, half, line, pcol]).astype(jnp.int32)

    own_panels = panels.reshape(supernodes, tile_rows, slice_rows, width)
    panel_pieces = []
    for dl in range(0, lines, 2):
        piece = own_panels if dl == 0 else move(own_panels, 0, 0, dl, 0)
        panel_pieces += [piece, move(piece, 0, 0, 1, 0)]
    by_half = sep_inverse.reshape(tile_rows, lines // 2, 2, 2, slice_rows, width)
    kept = lax.dynamic_index_in_dim(by_half, half, 2, keepdims=False).reshape(rows, width)
    given = lax.dynamic_index_in_dim(by_half, 1 - half, 2, keepdims=False).reshape(rows, width)
    sep_pieces, flips = [], []
    for dl in range(0, lines, 2):
        for dh in range(2):
            piece = kept if dl + dh == 0 else move((kept, given)[dh], 0, 0, dl, dh)
            sep_pieces += [piece, move(piece, 0, 0, 1, 0)]
            flips += [column_of(dl, dh), column_of(dl + 1, dh)]

    (stacked,) = call(
        functools.partial(inverse_kernel, supernodes=supernodes),
        [window_factor],
        0,
        [shape(window_factor.shape, f32)],
        [],
        cost=1_000_000_000,
    )
    (own_window,) = call(
        diagonal_kernel,
        [place, stacked, diag_inverse],
        1,
        [shape((rows_each, cols_each), f32)],
        [
            pltpu.VMEM((2, supernodes, width, width), f32),
            pltpu.VMEM((width, cols_each if 2 * cols_each == width else width), f32),
        ],
        cost=3_000_000_000,
    )

    high, low, *mine = call(
        functools.partial(
            products_kernel,
            pieces=lines,
            supernodes=supernodes,
            tile_rows=tile_rows,
            prow_count=prow_count,
        ),
        [after(place, own_window, sep_pieces[1], sep_pieces[3]), ancestors, *panel_pieces, stacked],
        2,
        [shape((supernodes, rows, width), bf16)] * 2
        + [shape((2, rows, block), bf16)] * (block == width),
        [pltpu.VMEM((supernodes, tile_rows, lines, slice_rows, width), f32)],
        cost=2_500_000_000,
    )
    if block == width:
        mine = mine[0]
    else:
        both = jnp.stack([high, low])
        slices = []
        for h in range(2):
            start = column_of(line, h) * cols_each
            chosen = lax.dynamic_index_in_dim(both, start // width, 1, keepdims=False)
            slices.append(lax.dynamic_slice_in_dim(chosen, start % width, cols_each, 2))
        mine = jnp.concatenate(slices, 2)
    mine = mine.reshape(2, tile_rows, lines, slice_rows, block)
    steps, lanes = [], []
    for dx, dh in sorted(((dx, dh) for dx in range(x_count) for dh in range(2)), key=lambda f: (f != (0, 0), -f[0] - f[1], f)):
        lanes.append(mine if dx + dh == 0 else move(mine, dx, 0, 0, dh))
        steps.append((dx, 0, dh))
    lanes[1:] = [after(lane, *sep_pieces[1:]) for lane in lanes[1:]]
    for (dx, _, dh), lane in zip(list(steps), list(lanes)):
        lanes.append(move(lane, 0, 1, 0, 0))
        steps.append((dx, 1, dh))

    kind = bf16 if slice_rows % 16 == 0 else f32
    *columns, sums_high, sums_low = call(
        functools.partial(
            columns_kernel,
            lanes=len(lanes),
            pieces=len(sep_pieces),
            lines=lines,
            prow_count=prow_count,
            width=width,
            steps=tuple(steps),
            flips=tuple(flips),
        ),
        [place, ancestors, *lanes, *sep_pieces],
        2,
        [shape((tile_rows, slice_rows, block), f32)] * lines + [shape((rows, block), bf16)] * 2,
        [
            pltpu.VMEM((2, tile_rows * prow_count, pcol_count, slice_rows, block), kind),
            pltpu.VMEM((tile_rows, lines, slice_rows, block), f32),
        ],
        cost=1_700_000_000,
    )
    column_pieces = [columns[0]] + [move(columns[d], 0, 0, d, 0) for d in range(1, lines)]
    keep, send = call(
        window_kernel,
        [place, high, low, sums_high, sums_low],
        1,
        [shape((x_count, 2, rows_each, cols_each), f32)] * 2,
        [pltpu.VMEM((order, block), f32)],
        cost=1_400_000_000,
    )
    received = move(send, 0, 1, 0, 0)
    parts = call(
        add_kernel,
        [keep, received],
        0,
        [shape((rows_each, cols_each), f32)] * (2 * x_count),
        [],
        cost=100_000_000,
    )
    by_node = block == width and lines == supernodes
    ys, done = call(
        ys_kernel,
        [place, *column_pieces],
        1,
        [
            shape((supernodes, tile_rows, slice_rows, width), f32)
            if by_node
            else shape((lines, 2, tile_rows, slice_rows, cols_each), f32),
            shape((8, 128), f32),
        ],
        [],
        cost=12_000_000_000,
        last=by_node,
    )
    if not by_node:
        ys = ys.reshape(lines // 2, 2, 2, tile_rows, slice_rows, cols_each)
        ys = jnp.transpose(ys, (3, 4, 0, 2, 1, 5))
        ys = ys.reshape(tile_rows, slice_rows, supernodes, width)
        ys = jnp.transpose(ys, (2, 0, 1, 3))
    summed = [parts[0]] + [
        move(parts[2 * dx + dh], dx, 0, 0, dh)
        for dx in range(x_count)
        for dh in range(2)
        if dx + dh > 0
    ]
    (window,) = call(
        last_kernel,
        [done, *summed, own_window],
        0,
        [shape((rows_each, cols_each), f32)],
        [],
        cost=500_000_000,
        last=True,
    )
    return ys.reshape(supernodes, tile_rows, 1, slice_rows, width), window


def solution(mesh):
    placed = (
        P(None, "prow", None, None, "pcol", None),
        P(None, None, "prow", "pcol", None),
        P(),
        P(),
        P(),
    )
    return jax.shard_map(
        per_device,
        mesh=mesh,
        in_specs=placed,
        out_specs=(P(None, None, "prow", "pcol", None), P("prow", "pcol")),
        check_vma=False,
    )
```

```python
import functools

import jax
import jax.numpy as jnp
from jax import lax
from jax.experimental import pallas as pl
from jax.experimental.pallas import tpu as pltpu
from jax.sharding import PartitionSpec as P

AXES = ("prow", "pcol")
HIGHEST = lax.Precision.HIGHEST
VMEM = pl.BlockSpec(memory_space=pltpu.VMEM)
SMEM = pl.BlockSpec(memory_space=pltpu.SMEM)


def pair_index(earlier, later):
    return later * (later - 1) // 2 + earlier


def exact_dot(left, right):
    return jnp.dot(left, right, precision=HIGHEST, preferred_element_type=jnp.float32)


def dot(left, right):
    return jnp.dot(left, right, preferred_element_type=jnp.float32)


def dot_rows(left, right):
    return lax.dot_general(
        left, right, (((0,), (0,)), ((), ())), preferred_element_type=jnp.float32
    )


def split(value):
    high = value.astype(jnp.bfloat16)
    return high, (value - high.astype(jnp.float32)).astype(jnp.bfloat16)


def column_of(line, half):
    return 4 * (line // 2) + 2 * half + line % 2


def move(value, dx, dc, dl, dh):
    prow_count, pcol_count = (lax.axis_size(a) for a in AXES)
    flip_row, flip_col = 2 * dx + dc, column_of(dl, dh)
    pairs = [
        (p * pcol_count + q, (p ^ flip_row) * pcol_count + (q ^ flip_col))
        for p in range(prow_count)
        for q in range(pcol_count)
    ]
    return lax.ppermute(value, AXES, pairs)


def exact_dot_rows(left, right):
    return lax.dot_general(
        left,
        right,
        (((0,), (0,)), ((), ())),
        precision=HIGHEST,
        preferred_element_type=jnp.float32,
    )


def three_parts(value):
    high, rest = split(value)
    low = (value - high.astype(jnp.float32) - rest.astype(jnp.float32)).astype(jnp.bfloat16)
    return high, rest, low


def inverse_kernel(factor_ref, inverse_ref, *, supernodes):
    for later in range(supernodes):
        for earlier in range(later):
            total = factor_ref[pair_index(earlier, later)].astype(jnp.float32)
            for middle in range(earlier + 1, later):
                right = factor_ref[pair_index(middle, later)]
                for part in three_parts(inverse_ref[pair_index(earlier, middle)]):
                    total = total + dot(part, right)
            inverse_ref[pair_index(earlier, later)] = -total


def diagonal_kernel(place_ref, inverse_ref, diag_ref, own_ref, full_ref, rows_ref):
    prow, pcol = place_ref[0], place_ref[5]
    supernodes, width, _ = diag_ref.shape
    rows_each, cols_each = own_ref.shape
    row_node, col_node = prow * rows_each // width, pcol * cols_each // width
    square = (width, width)
    on_diagonal = lax.broadcasted_iota(jnp.int32, square, 0) == lax.broadcasted_iota(
        jnp.int32, square, 1
    )
    for which, node in enumerate((row_node, col_node)):
        full_ref[which, node] = on_diagonal.astype(jnp.float32)

        @pl.loop(0, node)
        def _(k, which=which, node=node):
            full_ref[which, k] = inverse_ref[node * (node - 1) // 2 + k]

    halves = 2 * cols_each == width
    rows_ref[...] = jnp.zeros_like(rows_ref)

    @pl.loop(0, jnp.minimum(row_node, col_node) + 1)
    def _(k):
        cols = full_ref[1, k]
        if halves:
            cols = jnp.where(pcol % 2 == 0, cols[:, :cols_each], cols[:, cols_each:])
        scaled = sum(dot(diag_ref[k], part) for part in three_parts(cols))
        rows_ref[...] += exact_dot_rows(full_ref[0, k], scaled)

    first_row = pl.multiple_of(prow * rows_each % width, rows_each)
    rows = rows_ref[pl.ds(first_row, rows_each), :]
    if not halves:
        picked = lax.broadcasted_iota(jnp.int32, (width, cols_each), 0) == (
            lax.broadcasted_iota(jnp.int32, (width, cols_each), 1) + pcol * cols_each % width
        )
        rows = exact_dot(rows, picked.astype(jnp.float32))
    own_ref[...] = rows


def products_kernel(place_ref, flags_ref, *refs, pieces, supernodes, tile_rows, prow_count):
    panel_refs, inverse_ref = refs[:pieces], refs[pieces]
    high_ref, low_ref, *mine_refs, panel_ref = refs[pieces + 1 :]
    prow, line = place_ref[0], place_ref[4]
    for later in range(supernodes):
        for r in range(tile_rows):
            keep = flags_ref[later, r * prow_count + prow].astype(jnp.float32)
            for d in range(pieces):
                panel_ref[later, r, lax.bitwise_xor(line, d)] = (
                    panel_refs[d][later, r].astype(jnp.float32) * keep
                )
    rows, width = high_ref.shape[1], high_ref.shape[2]
    panels = [panel_ref[k].reshape(rows, width) for k in range(supernodes)]
    narrow = [panel.astype(jnp.bfloat16) for panel in panels]
    for later in range(supernodes):
        total = panels[later]
        for earlier in range(later):
            for part in split(inverse_ref[pair_index(earlier, later)]):
                total = total + dot(narrow[earlier], part)
        high_ref[later], low_ref[later] = split(total)
    for mine_ref in mine_refs:
        cols_each = width // 2
        first = line % 2 == 0
        for which, ref in enumerate((high_ref, low_ref)):
            for half in range(2):
                node = ref[column_of(line, half) // 2]
                mine_ref[which, :, half * cols_each : (half + 1) * cols_each] = jnp.where(
                    first, node[:, :cols_each], node[:, cols_each:]
                )


def columns_kernel(
    place_ref, flags_ref, *refs, lanes, pieces, lines, prow_count, width, steps, flips
):
    lane_refs, sep_refs = refs[:lanes], refs[lanes : lanes + pieces]
    column_refs = refs[lanes + pieces : lanes + pieces + lines]
    high_ref, low_ref, gathered_ref, sums_ref = refs[lanes + pieces + lines :]
    prow, x, core, half, line, pcol = (place_ref[i] for i in range(6))
    _, tile_rows, _, slice_rows, block = lane_refs[0].shape
    kind = gathered_ref.dtype
    for lane, (dx, dc, dh) in enumerate(steps):
        lane_prow = 2 * lax.bitwise_xor(x, dx) + lax.bitwise_xor(core, dc)
        lane_half = lax.bitwise_xor(half, dh)
        for which in range(2):
            for r in range(tile_rows):
                for sub in range(lines):
                    gathered_ref[
                        which, r * prow_count + lane_prow, column_of(sub, 0) + 2 * lane_half
                    ] = lane_refs[lane][which, r, sub].astype(kind)
    total = None
    for piece, flip in enumerate(flips):
        tile = lax.bitwise_xor(pcol, flip)
        sep = sep_refs[piece][...]
        for which in range(2):
            part = gathered_ref[which, tile].reshape(width, block).astype(jnp.bfloat16)
            term = dot(sep, part)
            total = term if total is None else total + term
    cols_each = block // 2
    nodes = [column_of(line, h) * cols_each // width for h in range(2)]
    sums_ref[...] = total.reshape(sums_ref.shape)
    first = lax.broadcasted_iota(jnp.int32, (slice_rows, block), 1) < cols_each
    for r in range(tile_rows):
        keeps = [flags_ref[k, r * prow_count + prow].astype(jnp.float32) for k in nodes]
        keep = jnp.where(first, -keeps[0], -keeps[1])
        for d in range(lines):
            column_refs[d][r] = sums_ref[r, lax.bitwise_xor(line, d)] * keep
    high_ref[...], low_ref[...] = split(total)


def window_kernel(
    place_ref, left_high_ref, left_low_ref, high_ref, low_ref, keep_ref, send_ref, window_ref
):
    x, core, half = (place_ref[i] for i in range(1, 4))
    supernodes, _, width = left_high_ref.shape
    high, low = high_ref[...], low_ref[...]
    block = high.shape[1]
    pair = jnp.concatenate([high, low], 1)
    for k in range(supernodes):
        both = dot_rows(left_high_ref[k], pair)
        window_ref[k * width : (k + 1) * width, :] = (
            both[:, :block] + both[:, block:] + dot_rows(left_low_ref[k], high)
        )
    x_count, _, rows_each, cols_each = keep_ref.shape
    for dx in range(x_count):
        for target, dc in ((keep_ref, 0), (send_ref, 1)):
            row_block = 2 * lax.bitwise_xor(x, dx) + lax.bitwise_xor(core, dc)
            rows = window_ref[pl.ds(pl.multiple_of(row_block * rows_each, rows_each), rows_each), :]
            first, second = rows[:, :cols_each], rows[:, cols_each:]
            target[dx, 0] = jnp.where(half == 0, first, second)
            target[dx, 1] = jnp.where(half == 0, second, first)


def add_kernel(keep_ref, received_ref, *out_refs):
    x_count = keep_ref.shape[0]
    for dx in range(x_count):
        for dy in range(2):
            out_refs[2 * dx + dy][...] = keep_ref[dx, dy] + received_ref[dx, dy]


def last_kernel(_, *refs):
    *part_refs, window_ref = refs
    total = part_refs[0][...]
    for ref in part_refs[1:]:
        total = total + ref[...]
    window_ref[...] = total


def ys_kernel(place_ref, *refs):
    *column_refs, ys_ref, done_ref = refs
    done_ref[...] = jnp.zeros_like(done_ref)
    line = place_ref[4]
    block = column_refs[0].shape[2]
    cols_each = block // 2
    if ys_ref.ndim == 4 and ys_ref.shape[0] == len(column_refs) and ys_ref.shape[3] == block:
        first = line % 2 == 0
        for d in range(0, len(column_refs), 2):
            for half in range(2):
                node = column_of(lax.bitwise_xor(line, d), half) // 2
                cols = slice(half * cols_each, (half + 1) * cols_each)
                even, odd = column_refs[d][:, :, cols], column_refs[d + 1][:, :, cols]
                ys_ref[node, :, :, :cols_each] = jnp.where(first, even, odd)
                ys_ref[node, :, :, cols_each:] = jnp.where(first, odd, even)
    else:
        for d, ref in enumerate(column_refs):
            for half in range(2):
                ys_ref[lax.bitwise_xor(line, d), half] = ref[
                    :, :, half * cols_each : (half + 1) * cols_each
                ]


def after(value, *others):
    return lax.optimization_barrier((value, *others))[0]


def call(kernel, operands, scalars, outs, scratch, cost, last=False):
    arrays = [pltpu.with_memory_space_constraint(a, pltpu.VMEM) for a in operands[scalars:]]
    return pl.pallas_call(
        kernel,
        out_shape=outs if last else [pltpu.VMEM(out.shape, out.dtype) for out in outs],
        in_specs=[SMEM] * scalars + [VMEM] * len(arrays),
        out_specs=[VMEM] * len(outs),
        scratch_shapes=scratch,
        compiler_params=pltpu.CompilerParams(vmem_limit_bytes=20 * 1024 * 1024),
        cost_estimate=pl.CostEstimate(flops=cost, bytes_accessed=0, transcendentals=0),
    )(*operands[:scalars], *arrays)


def per_device(sep_inverse, panels, ancestors, window_factor, diag_inverse):
    prow_count, pcol_count = (lax.axis_size(a) for a in AXES)
    prow, pcol = (lax.axis_index(a) for a in AXES)
    x_count, lines = prow_count // 2, pcol_count // 2
    x, core, half = prow // 2, prow % 2, pcol // 2 % 2
    line = 2 * (pcol // 4) + pcol % 2
    tile_rows, width = sep_inverse.shape[0], sep_inverse.shape[2]
    supernodes, slice_rows = panels.shape[0], panels.shape[3]
    order = supernodes * width
    rows_each, cols_each = order // prow_count, order // pcol_count
    block = 2 * cols_each
    rows = tile_rows * lines * slice_rows
    bf16, f32 = jnp.bfloat16, jnp.float32
    shape = jax.ShapeDtypeStruct
    place = jnp.stack([prow, x, core, half, line, pcol]).astype(jnp.int32)

    own_panels = panels.reshape(supernodes, tile_rows, slice_rows, width)
    panel_pieces = []
    for dl in range(0, lines, 2):
        piece = own_panels if dl == 0 else move(own_panels, 0, 0, dl, 0)
        panel_pieces += [piece, move(piece, 0, 0, 1, 0)]
    by_half = sep_inverse.reshape(tile_rows, lines // 2, 2, 2, slice_rows, width)
    kept = lax.dynamic_index_in_dim(by_half, half, 2, keepdims=False).reshape(rows, width)
    given = lax.dynamic_index_in_dim(by_half, 1 - half, 2, keepdims=False).reshape(rows, width)
    sep_pieces, flips = [], []
    for dl in range(0, lines, 2):
        for dh in range(2):
            piece = kept if dl + dh == 0 else move((kept, given)[dh], 0, 0, dl, dh)
            sep_pieces += [piece, move(piece, 0, 0, 1, 0)]
            flips += [column_of(dl, dh), column_of(dl + 1, dh)]

    (stacked,) = call(
        functools.partial(inverse_kernel, supernodes=supernodes),
        [window_factor],
        0,
        [shape(window_factor.shape, f32)],
        [],
        cost=1_000_000_000,
    )
    (own_window,) = call(
        diagonal_kernel,
        [place, stacked, diag_inverse],
        1,
        [shape((rows_each, cols_each), f32)],
        [
            pltpu.VMEM((2, supernodes, width, width), f32),
            pltpu.VMEM((width, cols_each if 2 * cols_each == width else width), f32),
        ],
        cost=3_000_000_000,
    )

    high, low, *mine = call(
        functools.partial(
            products_kernel,
            pieces=lines,
            supernodes=supernodes,
            tile_rows=tile_rows,
            prow_count=prow_count,
        ),
        [after(place, own_window, sep_pieces[1], sep_pieces[3]), ancestors, *panel_pieces, stacked],
        2,
        [shape((supernodes, rows, width), bf16)] * 2
        + [shape((2, rows, block), bf16)] * (block == width),
        [pltpu.VMEM((supernodes, tile_rows, lines, slice_rows, width), f32)],
        cost=2_500_000_000,
    )
    if block == width:
        mine = mine[0]
    else:
        both = jnp.stack([high, low])
        slices = []
        for h in range(2):
            start = column_of(line, h) * cols_each
            chosen = lax.dynamic_index_in_dim(both, start // width, 1, keepdims=False)
            slices.append(lax.dynamic_slice_in_dim(chosen, start % width, cols_each, 2))
        mine = jnp.concatenate(slices, 2)
    mine = mine.reshape(2, tile_rows, lines, slice_rows, block)
    steps, lanes = [], []
    for dx, dh in sorted(((dx, dh) for dx in range(x_count) for dh in range(2)), key=lambda f: (f != (0, 0), -f[0] - f[1], f)):
        lanes.append(mine if dx + dh == 0 else move(mine, dx, 0, 0, dh))
        steps.append((dx, 0, dh))
    lanes[1:] = [after(lane, *sep_pieces[1:]) for lane in lanes[1:]]
    for (dx, _, dh), lane in zip(list(steps), list(lanes)):
        lanes.append(move(lane, 0, 1, 0, 0))
        steps.append((dx, 1, dh))

    kind = bf16 if slice_rows % 16 == 0 else f32
    *columns, sums_high, sums_low = call(
        functools.partial(
            columns_kernel,
            lanes=len(lanes),
            pieces=len(sep_pieces),
            lines=lines,
            prow_count=prow_count,
            width=width,
            steps=tuple(steps),
            flips=tuple(flips),
        ),
        [place, ancestors, *lanes, *sep_pieces],
        2,
        [shape((tile_rows, slice_rows, block), f32)] * lines + [shape((rows, block), bf16)] * 2,
        [
            pltpu.VMEM((2, tile_rows * prow_count, pcol_count, slice_rows, block), kind),
            pltpu.VMEM((tile_rows, lines, slice_rows, block), f32),
        ],
        cost=1_700_000_000,
    )
    column_pieces = [columns[0]] + [move(columns[d], 0, 0, d, 0) for d in range(1, lines)]
    keep, send = call(
        window_kernel,
        [place, high, low, sums_high, sums_low],
        1,
        [shape((x_count, 2, rows_each, cols_each), f32)] * 2,
        [pltpu.VMEM((order, block), f32)],
        cost=1_400_000_000,
    )
    received = move(send, 0, 1, 0, 0)
    parts = call(
        add_kernel,
        [keep, received],
        0,
        [shape((rows_each, cols_each), f32)] * (2 * x_count),
        [],
        cost=100_000_000,
    )
    by_node = block == width and lines == supernodes
    ys, done = call(
        ys_kernel,
        [place, *column_pieces],
        1,
        [
            shape((supernodes, tile_rows, slice_rows, width), f32)
            if by_node
            else shape((lines, 2, tile_rows, slice_rows, cols_each), f32),
            shape((8, 128), f32),
        ],
        [],
        cost=12_000_000_000,
        last=by_node,
    )
    if not by_node:
        ys = ys.reshape(lines // 2, 2, 2, tile_rows, slice_rows, cols_each)
        ys = jnp.transpose(ys, (3, 4, 0, 2, 1, 5))
        ys = ys.reshape(tile_rows, slice_rows, supernodes, width)
        ys = jnp.transpose(ys, (2, 0, 1, 3))
    summed = [parts[0]] + [
        move(parts[2 * dx + dh], dx, 0, 0, dh)
        for dx in range(x_count)
        for dh in range(2)
        if dx + dh > 0
    ]
    (window,) = call(
        last_kernel,
        [done, *summed, own_window],
        0,
        [shape((rows_each, cols_each), f32)],
        [],
        cost=500_000_000,
        last=True,
    )
    return ys.reshape(supernodes, tile_rows, 1, slice_rows, width), window


def solution(mesh):
    placed = (
        P(None, "prow", None, None, "pcol", None),
        P(None, None, "prow", "pcol", None),
        P(),
        P(),
        P(),
    )
    return jax.shard_map(
        per_device,
        mesh=mesh,
        in_specs=placed,
        out_specs=(P(None, None, "prow", "pcol", None), P("prow", "pcol")),
        check_vma=False,
    )
```

```python
import functools

import jax
import jax.numpy as jnp
from jax import lax
from jax.experimental import pallas as pl
from jax.experimental.pallas import tpu as pltpu
from jax.sharding import PartitionSpec as P

AXES = ("prow", "pcol")
HIGHEST = lax.Precision.HIGHEST
VMEM = pl.BlockSpec(memory_space=pltpu.VMEM)
SMEM = pl.BlockSpec(memory_space=pltpu.SMEM)


def pair_index(earlier, later):
    return later * (later - 1) // 2 + earlier


def exact_dot(left, right):
    return jnp.dot(left, right, precision=HIGHEST, preferred_element_type=jnp.float32)


def dot(left, right):
    return jnp.dot(left, right, preferred_element_type=jnp.float32)


def dot_rows(left, right):
    return lax.dot_general(
        left, right, (((0,), (0,)), ((), ())), preferred_element_type=jnp.float32
    )


def split(value):
    high = value.astype(jnp.bfloat16)
    return high, (value - high.astype(jnp.float32)).astype(jnp.bfloat16)


def column_of(line, half):
    return 4 * (line // 2) + 2 * half + line % 2


def move(value, dx, dc, dl, dh):
    prow_count, pcol_count = (lax.axis_size(a) for a in AXES)
    flip_row, flip_col = 2 * dx + dc, column_of(dl, dh)
    pairs = [
        (p * pcol_count + q, (p ^ flip_row) * pcol_count + (q ^ flip_col))
        for p in range(prow_count)
        for q in range(pcol_count)
    ]
    return lax.ppermute(value, AXES, pairs)


def exact_dot_rows(left, right):
    return lax.dot_general(
        left,
        right,
        (((0,), (0,)), ((), ())),
        precision=HIGHEST,
        preferred_element_type=jnp.float32,
    )


def three_parts(value):
    high, rest = split(value)
    low = (value - high.astype(jnp.float32) - rest.astype(jnp.float32)).astype(jnp.bfloat16)
    return high, rest, low


def inverse_kernel(factor_ref, inverse_ref, *, supernodes):
    for later in range(supernodes):
        for earlier in range(later):
            total = factor_ref[pair_index(earlier, later)].astype(jnp.float32)
            for middle in range(earlier + 1, later):
                right = factor_ref[pair_index(middle, later)]
                for part in three_parts(inverse_ref[pair_index(earlier, middle)]):
                    total = total + dot(part, right)
            inverse_ref[pair_index(earlier, later)] = -total


def diagonal_kernel(place_ref, inverse_ref, diag_ref, own_ref, full_ref, rows_ref):
    prow, pcol = place_ref[0], place_ref[5]
    supernodes, width, _ = diag_ref.shape
    rows_each, cols_each = own_ref.shape
    row_node, col_node = prow * rows_each // width, pcol * cols_each // width
    square = (width, width)
    on_diagonal = lax.broadcasted_iota(jnp.int32, square, 0) == lax.broadcasted_iota(
        jnp.int32, square, 1
    )
    for which, node in enumerate((row_node, col_node)):
        full_ref[which, node] = on_diagonal.astype(jnp.float32)

        @pl.loop(0, node)
        def _(k, which=which, node=node):
            full_ref[which, k] = inverse_ref[node * (node - 1) // 2 + k]

    halves = 2 * cols_each == width
    rows_ref[...] = jnp.zeros_like(rows_ref)

    @pl.loop(0, jnp.minimum(row_node, col_node) + 1)
    def _(k):
        cols = full_ref[1, k]
        if halves:
            cols = jnp.where(pcol % 2 == 0, cols[:, :cols_each], cols[:, cols_each:])
        scaled = sum(dot(diag_ref[k], part) for part in three_parts(cols))
        rows_ref[...] += exact_dot_rows(full_ref[0, k], scaled)

    first_row = pl.multiple_of(prow * rows_each % width, rows_each)
    rows = rows_ref[pl.ds(first_row, rows_each), :]
    if not halves:
        picked = lax.broadcasted_iota(jnp.int32, (width, cols_each), 0) == (
            lax.broadcasted_iota(jnp.int32, (width, cols_each), 1) + pcol * cols_each % width
        )
        rows = exact_dot(rows, picked.astype(jnp.float32))
    own_ref[...] = rows


def products_kernel(place_ref, flags_ref, *refs, pieces, supernodes, tile_rows, prow_count):
    panel_refs, inverse_ref = refs[:pieces], refs[pieces]
    high_ref, low_ref, *mine_refs, panel_ref = refs[pieces + 1 :]
    prow, line = place_ref[0], place_ref[4]
    for later in range(supernodes):
        for r in range(tile_rows):
            keep = flags_ref[later, r * prow_count + prow].astype(jnp.float32)
            for d in range(pieces):
                panel_ref[later, r, lax.bitwise_xor(line, d)] = (
                    panel_refs[d][later, r].astype(jnp.float32) * keep
                )
    rows, width = high_ref.shape[1], high_ref.shape[2]
    panels = [panel_ref[k].reshape(rows, width) for k in range(supernodes)]
    narrow = [panel.astype(jnp.bfloat16) for panel in panels]
    for later in range(supernodes):
        total = panels[later]
        for earlier in range(later):
            for part in split(inverse_ref[pair_index(earlier, later)]):
                total = total + dot(narrow[earlier], part)
        high_ref[later], low_ref[later] = split(total)
    for mine_ref in mine_refs:
        cols_each = width // 2
        first = line % 2 == 0
        for which, ref in enumerate((high_ref, low_ref)):
            for half in range(2):
                node = ref[column_of(line, half) // 2]
                mine_ref[which, :, half * cols_each : (half + 1) * cols_each] = jnp.where(
                    first, node[:, :cols_each], node[:, cols_each:]
                )


def columns_kernel(
    place_ref, flags_ref, *refs, lanes, pieces, lines, prow_count, width, steps, flips
):
    lane_refs, sep_refs = refs[:lanes], refs[lanes : lanes + pieces]
    column_refs = refs[lanes + pieces : lanes + pieces + lines]
    high_ref, low_ref, gathered_ref, sums_ref = refs[lanes + pieces + lines :]
    prow, x, core, half, line, pcol = (place_ref[i] for i in range(6))
    _, tile_rows, _, slice_rows, block = lane_refs[0].shape
    kind = gathered_ref.dtype
    for lane, (dx, dc, dh) in enumerate(steps):
        lane_prow = 2 * lax.bitwise_xor(x, dx) + lax.bitwise_xor(core, dc)
        lane_half = lax.bitwise_xor(half, dh)
        for which in range(2):
            for r in range(tile_rows):
                for sub in range(lines):
                    gathered_ref[
                        which, r * prow_count + lane_prow, column_of(sub, 0) + 2 * lane_half
                    ] = lane_refs[lane][which, r, sub].astype(kind)
    total = None
    for piece, flip in enumerate(flips):
        tile = lax.bitwise_xor(pcol, flip)
        sep = sep_refs[piece][...]
        for which in range(2):
            part = gathered_ref[which, tile].reshape(width, block).astype(jnp.bfloat16)
            term = dot(sep, part)
            total = term if total is None else total + term
    cols_each = block // 2
    nodes = [column_of(line, h) * cols_each // width for h in range(2)]
    sums_ref[...] = total.reshape(sums_ref.shape)
    first = lax.broadcasted_iota(jnp.int32, (slice_rows, block), 1) < cols_each
    for r in range(tile_rows):
        keeps = [flags_ref[k, r * prow_count + prow].astype(jnp.float32) for k in nodes]
        keep = jnp.where(first, -keeps[0], -keeps[1])
        for d in range(lines):
            column_refs[d][r] = sums_ref[r, lax.bitwise_xor(line, d)] * keep
    high_ref[...], low_ref[...] = split(total)


def window_kernel(
    place_ref, left_high_ref, left_low_ref, high_ref, low_ref, keep_ref, send_ref, window_ref
):
    x, core, half = (place_ref[i] for i in range(1, 4))
    supernodes, _, width = left_high_ref.shape
    high, low = high_ref[...], low_ref[...]
    block = high.shape[1]
    pair = jnp.concatenate([high, low], 1)
    x_count, _, cols_each, rows_each = keep_ref.shape
    for k in range(supernodes):
        both = dot_rows(pair, left_high_ref[k])
        total = both[:block] + both[block:] + dot_rows(high, left_low_ref[k])
        for first in range(0, width, rows_each):
            window_ref[(k * width + first) // rows_each] = total[:, first : first + rows_each]
    for dx in range(x_count):
        for target, dc in ((keep_ref, 0), (send_ref, 1)):
            part = window_ref[2 * lax.bitwise_xor(x, dx) + lax.bitwise_xor(core, dc)]
            first, second = part[:cols_each], part[cols_each:]
            target[dx, 0] = jnp.where(half == 0, first, second)
            target[dx, 1] = jnp.where(half == 0, second, first)


def add_kernel(keep_ref, received_ref, *out_refs):
    x_count = keep_ref.shape[0]
    for dx in range(x_count):
        for dy in range(2):
            out_refs[2 * dx + dy][...] = keep_ref[dx, dy] + received_ref[dx, dy]


def last_kernel(_, *refs):
    *part_refs, own_ref, window_ref = refs
    total = part_refs[0][...]
    for ref in part_refs[1:]:
        total = total + ref[...]
    window_ref[...] = total.T + own_ref[...]


def ys_kernel(place_ref, *refs):
    *column_refs, ys_ref, done_ref = refs
    done_ref[...] = jnp.zeros_like(done_ref)
    line = place_ref[4]
    block = column_refs[0].shape[2]
    cols_each = block // 2
    if ys_ref.ndim == 4 and ys_ref.shape[0] == len(column_refs) and ys_ref.shape[3] == block:
        first = line % 2 == 0
        for d in range(0, len(column_refs), 2):
            for half in range(2):
                node = column_of(lax.bitwise_xor(line, d), half) // 2
                cols = slice(half * cols_each, (half + 1) * cols_each)
                even, odd = column_refs[d][:, :, cols], column_refs[d + 1][:, :, cols]
                ys_ref[node, :, :, :cols_each] = jnp.where(first, even, odd)
                ys_ref[node, :, :, cols_each:] = jnp.where(first, odd, even)
    else:
        for d, ref in enumerate(column_refs):
            for half in range(2):
                ys_ref[lax.bitwise_xor(line, d), half] = ref[
                    :, :, half * cols_each : (half + 1) * cols_each
                ]


def after(value, *others):
    return lax.optimization_barrier((value, *others))[0]


def call(kernel, operands, scalars, outs, scratch, cost, last=False):
    arrays = [pltpu.with_memory_space_constraint(a, pltpu.VMEM) for a in operands[scalars:]]
    return pl.pallas_call(
        kernel,
        out_shape=outs if last else [pltpu.VMEM(out.shape, out.dtype) for out in outs],
        in_specs=[SMEM] * scalars + [VMEM] * len(arrays),
        out_specs=[VMEM] * len(outs),
        scratch_shapes=scratch,
        compiler_params=pltpu.CompilerParams(vmem_limit_bytes=20 * 1024 * 1024),
        cost_estimate=pl.CostEstimate(flops=cost, bytes_accessed=0, transcendentals=0),
    )(*operands[:scalars], *arrays)


def per_device(sep_inverse, panels, ancestors, window_factor, diag_inverse):
    prow_count, pcol_count = (lax.axis_size(a) for a in AXES)
    prow, pcol = (lax.axis_index(a) for a in AXES)
    x_count, lines = prow_count // 2, pcol_count // 2
    x, core, half = prow // 2, prow % 2, pcol // 2 % 2
    line = 2 * (pcol // 4) + pcol % 2
    tile_rows, width = sep_inverse.shape[0], sep_inverse.shape[2]
    supernodes, slice_rows = panels.shape[0], panels.shape[3]
    order = supernodes * width
    rows_each, cols_each = order // prow_count, order // pcol_count
    block = 2 * cols_each
    rows = tile_rows * lines * slice_rows
    bf16, f32 = jnp.bfloat16, jnp.float32
    shape = jax.ShapeDtypeStruct
    place = jnp.stack([prow, x, core, half, line, pcol]).astype(jnp.int32)

    own_panels = panels.reshape(supernodes, tile_rows, slice_rows, width)
    panel_pieces = []
    for dl in range(0, lines, 2):
        piece = own_panels if dl == 0 else move(own_panels, 0, 0, dl, 0)
        panel_pieces += [piece, move(piece, 0, 0, 1, 0)]
    by_half = sep_inverse.reshape(tile_rows, lines // 2, 2, 2, slice_rows, width)
    kept = lax.dynamic_index_in_dim(by_half, half, 2, keepdims=False).reshape(rows, width)
    given = lax.dynamic_index_in_dim(by_half, 1 - half, 2, keepdims=False).reshape(rows, width)
    sep_pieces, flips = [], []
    for dl in range(0, lines, 2):
        for dh in range(2):
            piece = kept if dl + dh == 0 else move((kept, given)[dh], 0, 0, dl, dh)
            sep_pieces += [piece, move(piece, 0, 0, 1, 0)]
            flips += [column_of(dl, dh), column_of(dl + 1, dh)]

    (stacked,) = call(
        functools.partial(inverse_kernel, supernodes=supernodes),
        [window_factor],
        0,
        [shape(window_factor.shape, f32)],
        [],
        cost=1_000_000_000,
    )
    (own_window,) = call(
        diagonal_kernel,
        [place, stacked, diag_inverse],
        1,
        [shape((rows_each, cols_each), f32)],
        [
            pltpu.VMEM((2, supernodes, width, width), f32),
            pltpu.VMEM((width, cols_each if 2 * cols_each == width else width), f32),
        ],
        cost=3_000_000_000,
    )

    high, low, *mine = call(
        functools.partial(
            products_kernel,
            pieces=lines,
            supernodes=supernodes,
            tile_rows=tile_rows,
            prow_count=prow_count,
        ),
        [after(place, own_window, sep_pieces[1], sep_pieces[3]), ancestors, *panel_pieces, stacked],
        2,
        [shape((supernodes, rows, width), bf16)] * 2
        + [shape((2, rows, block), bf16)] * (block == width),
        [pltpu.VMEM((supernodes, tile_rows, lines, slice_rows, width), f32)],
        cost=2_500_000_000,
    )
    if block == width:
        mine = mine[0]
    else:
        both = jnp.stack([high, low])
        slices = []
        for h in range(2):
            start = column_of(line, h) * cols_each
            chosen = lax.dynamic_index_in_dim(both, start // width, 1, keepdims=False)
            slices.append(lax.dynamic_slice_in_dim(chosen, start % width, cols_each, 2))
        mine = jnp.concatenate(slices, 2)
    mine = mine.reshape(2, tile_rows, lines, slice_rows, block)
    steps, lanes = [], []
    for dx, dh in sorted(((dx, dh) for dx in range(x_count) for dh in range(2)), key=lambda f: (f != (0, 0), -f[0] - f[1], f)):
        lanes.append(mine if dx + dh == 0 else move(mine, dx, 0, 0, dh))
        steps.append((dx, 0, dh))
    lanes[1:] = [after(lane, *sep_pieces[1:]) for lane in lanes[1:]]
    for (dx, _, dh), lane in zip(list(steps), list(lanes)):
        lanes.append(move(lane, 0, 1, 0, 0))
        steps.append((dx, 1, dh))

    kind = bf16 if slice_rows % 16 == 0 else f32
    *columns, sums_high, sums_low = call(
        functools.partial(
            columns_kernel,
            lanes=len(lanes),
            pieces=len(sep_pieces),
            lines=lines,
            prow_count=prow_count,
            width=width,
            steps=tuple(steps),
            flips=tuple(flips),
        ),
        [place, ancestors, *lanes, *sep_pieces],
        2,
        [shape((tile_rows, slice_rows, block), f32)] * lines + [shape((rows, block), bf16)] * 2,
        [
            pltpu.VMEM((2, tile_rows * prow_count, pcol_count, slice_rows, block), kind),
            pltpu.VMEM((tile_rows, lines, slice_rows, block), f32),
        ],
        cost=1_700_000_000,
    )
    column_pieces = [columns[0]] + [move(columns[d], 0, 0, d, 0) for d in range(1, lines)]
    keep, send = call(
        window_kernel,
        [place, high, low, sums_high, sums_low],
        1,
        [shape((x_count, 2, cols_each, rows_each), f32)] * 2,
        [pltpu.VMEM((prow_count, block, rows_each), f32)],
        cost=1_400_000_000,
    )
    received = move(send, 0, 1, 0, 0)
    parts = call(
        add_kernel,
        [keep, received],
        0,
        [shape((cols_each, rows_each), f32)] * (2 * x_count),
        [],
        cost=100_000_000,
    )
    by_node = block == width and lines == supernodes
    ys, done = call(
        ys_kernel,
        [place, *column_pieces],
        1,
        [
            shape((supernodes, tile_rows, slice_rows, width), f32)
            if by_node
            else shape((lines, 2, tile_rows, slice_rows, cols_each), f32),
            shape((8, 128), f32),
        ],
        [],
        cost=12_000_000_000,
        last=by_node,
    )
    if not by_node:
        ys = ys.reshape(lines // 2, 2, 2, tile_rows, slice_rows, cols_each)
        ys = jnp.transpose(ys, (3, 4, 0, 2, 1, 5))
        ys = ys.reshape(tile_rows, slice_rows, supernodes, width)
        ys = jnp.transpose(ys, (2, 0, 1, 3))
    summed = [parts[0]] + [
        move(parts[2 * dx + dh], dx, 0, 0, dh)
        for dx in range(x_count)
        for dh in range(2)
        if dx + dh > 0
    ]
    (window,) = call(
        last_kernel,
        [done, *summed, own_window],
        0,
        [shape((rows_each, cols_each), f32)],
        [],
        cost=500_000_000,
        last=True,
    )
    return ys.reshape(supernodes, tile_rows, 1, slice_rows, width), window


def solution(mesh):
    placed = (
        P(None, "prow", None, None, "pcol", None),
        P(None, None, "prow", "pcol", None),
        P(),
        P(),
        P(),
    )
    return jax.shard_map(
        per_device,
        mesh=mesh,
        in_specs=placed,
        out_specs=(P(None, None, "prow", "pcol", None), P("prow", "pcol")),
        check_vma=False,
    )
```
